32 devices in a mesh: row: 8 (over z, x), col: 4 (over y, core).
Axes of the slice: x: 2, y: 2, z: 4, core: 2. Of those that a mesh axis runs over, the one named last changes fastest.
Arguments:
- tile_vals: bfloat16 [8, 4, 256, 128, 128], P('row', 'col'), may hold values from -0.125 to 0.125
- tile_row: int32 [8, 4, 256], P('row', 'col'), may hold values from 0 to 15
- tile_col: int32 [8, 4, 256], P('row', 'col'), may hold values from 0 to 31
- tile_count: int32 [8, 4], P('row', 'col'), may hold values from 64 to 256
- out_grad: bfloat16 [16384, 128], P('row', 'col'), may hold values from -6 to 6
- relu_mask: int32 [16384, 128], P('row', 'col'), may hold values 0 or 1
- features: bfloat16 [16384, 128], P(('row', 'col')), may hold values from -6 to 6
- weight: bfloat16 [128, 128], replicated, may hold values from -0.5 to 0.5
- importance: float32 [128, 128], replicated, may hold values from 0 to 1
- weight_delta: float32 [128, 128], replicated, may hold values from -0.046875 to 0.046875
Outputs:
- input_grad: bfloat16 [16384, 128], P(('row', 'col'))
- importance_out: float32 [128, 128], replicated
The draws below stay inside these ranges and needn't reach their ends.
All inputs are finite; a program needn't handle non-finite values. No bound on the sum of `relu_mask` on one device may be relied on, other than what follows from the above.
Results may differ from the reference program's by a relative error of at most 0.022.
Values may be sent and summed in bfloat16 or wider, within the bound.
A program may use at most 128 MiB of HBM per device.

```python
import jax
import jax.numpy as jnp
from jax import lax

F = 128
D_IN = 128
TILE = 128
NB = 512
TILES = 256
NODES = 16384
ROWT = 16
COLT = 32
N_ROW = 8
N_COL = 4


def draw_tile_count(key, part):
    key = jax.random.fold_in(key, 7)
    first_key, second_key = jax.random.split(key)
    counts = jax.random.randint(first_key, (N_ROW, N_COL), TILES // 4, TILES + 1)
    chosen = jax.random.randint(second_key, (), 0, N_ROW * N_COL)
    flat_counts = counts.reshape(-1).at[chosen].set(TILES)
    return flat_counts.reshape(N_ROW, N_COL).astype(jnp.int32)


def with_ends(drawn, stream_key, smallest, largest):
    place = [jax.random.randint(jax.random.fold_in(stream_key, axis), (), 0, length) for axis, length in enumerate(drawn.shape)]
    longest = drawn.shape.index(max(drawn.shape))
    beside = place[:longest] + [(place[longest] + 1) % drawn.shape[longest]] + place[longest + 1:]
    return drawn.at[tuple(place)].set(smallest).at[tuple(beside)].set(largest)


def levels(stream_key, dims, shards, low, top_value):
    loudness, own = 1.0, jax.random.fold_in(stream_key, 6)
    for position, shards_of in shards:
        steps = jnp.exp(jax.random.uniform(jax.random.fold_in(own, position), (shards_of,), jnp.float32, low / len(shards), top_value / len(shards)))
        loudness = loudness * jnp.repeat(steps, dims[position] // shards_of).reshape([-1 if axis == position else 1 for axis in range(len(dims))])
    return loudness


def gaussian(key, dims, deviation, most, pieces=(), kind=jnp.bfloat16):
    result = deviation * jax.random.normal(key, dims, jnp.float32)
    if pieces:
        result = result * levels(key, dims, pieces, -0.22, 0.18)
    return jnp.clip(result, -most, most).astype(kind)


def setup_inputs(seed: int = 0) -> dict:
    key_of = jax.random.split(jax.random.key(seed), 11)
    return {
        "tile_vals": gaussian(key_of[0], (N_ROW, N_COL, TILES, TILE, TILE), (TILE * TILES * 2 // COLT) ** -0.5, 0.125, ((0, 8), (1, 4))),
        "tile_row": with_ends(jax.random.randint(key_of[1], (N_ROW, N_COL, TILES), 0, ROWT), jax.random.fold_in(key_of[1], 1), 0, ROWT - 1).astype(jnp.int32),
        "tile_col": with_ends(jax.random.randint(key_of[2], (N_ROW, N_COL, TILES), 0, COLT), jax.random.fold_in(key_of[2], 1), 0, COLT - 1).astype(jnp.int32),
        "tile_count": draw_tile_count(jax.random.fold_in(key_of[10], 71), 0),
        "out_grad": gaussian(key_of[4], (NODES, F), 1.0, 6.0, ((0, 8), (1, 4))),
        "relu_mask": with_ends((jax.random.randint(key_of[5], (NODES, F), 0, 2) < 1).astype(jnp.int32), jax.random.fold_in(key_of[5], 1), 0, 1),
        "features": gaussian(key_of[6], (NODES, D_IN), 1.0, 6.0, ((0, 32),)),
        "weight": gaussian(key_of[7], (D_IN, F), F ** -0.5, 0.5),
        "importance": jnp.clip(jax.random.uniform(key_of[8], (D_IN, F), jnp.float32, 0.0, 1.0), 0.0, 1.0),
        "weight_delta": gaussian(key_of[9], (D_IN, F), (NODES ** -0.5), 0.046875, (), jnp.float32),
    }


def reference(tile_vals, tile_row, tile_col, tile_count, out_grad, relu_mask, features, weight, importance, weight_delta):
    masked = (out_grad.astype(jnp.float32) * relu_mask.astype(jnp.float32)).astype(jnp.bfloat16)
    row_blocks = masked.reshape(N_ROW, ROWT, TILE, F)
    flat_vals = tile_vals.reshape(N_ROW * N_COL, TILES, TILE, TILE)
    flat_rows = tile_row.reshape(N_ROW * N_COL, TILES)
    flat_cols = tile_col.reshape(N_ROW * N_COL, TILES)
    flat_count = tile_count.reshape(N_ROW * N_COL)
    per_block = NB // TILE
    column_index = jnp.arange(COLT, dtype=jnp.int32)

    def device_step(aggregate, device):
        row_pos = device // N_COL
        col_pos = device % N_COL
        picked = row_blocks[row_pos][flat_rows[device]]
        product = jnp.einsum("tij,tif->tjf", flat_vals[device].astype(jnp.float32), picked.astype(jnp.float32))
        usable = (jnp.arange(TILES, dtype=jnp.int32) < flat_count[device]).astype(jnp.float32)
        product = product * usable[:, None, None]
        partial_value = jnp.zeros((COLT, TILE, F), jnp.float32).at[flat_cols[device]].add(product)
        partial_b = lax.optimization_barrier(partial_value.astype(jnp.bfloat16)).astype(jnp.float32)
        target = ((column_index * TILE) // NB * N_COL + col_pos) * per_block + ((column_index * TILE) % NB) // TILE
        aggregate = aggregate.at[target.astype(jnp.int32)].add(partial_b)
        return aggregate, None

    start_agg = jnp.zeros((NODES // TILE, TILE, F), jnp.float32)
    aggregate, _ = lax.scan(device_step, start_agg, jnp.arange(N_ROW * N_COL, dtype=jnp.int32))
    aggregate_b = aggregate.reshape(NODES, F).astype(jnp.bfloat16)
    input_grad = jnp.dot(aggregate_b, weight.T, preferred_element_type=jnp.float32).astype(jnp.bfloat16)
    weight_grad = jnp.dot(features.T, aggregate_b, preferred_element_type=jnp.float32)
    importance_out = importance - weight_grad * weight_delta
    return input_grad, importance_out
```

```python
import functools

import jax
import jax.numpy as jnp
from jax import lax
from jax.experimental import pallas as pl
from jax.experimental.pallas import tpu as pltpu
from jax.sharding import PartitionSpec as P

MESH = pl.DeviceIdType.MESH
VMEM = pl.BlockSpec(memory_space=pltpu.VMEM)
SMEM = pl.BlockSpec(memory_space=pltpu.SMEM)


def remote(src, dst, send_sem, recv_sem, device):
    return pltpu.make_async_remote_copy(
        src_ref=src,
        dst_ref=dst,
        send_sem=send_sem,
        recv_sem=recv_sem,
        device_id=device,
        device_id_type=MESH,
    )


def greet(devices):
    barrier = pltpu.get_barrier_semaphore()
    for device in devices:
        pl.semaphore_signal(barrier, inc=1, device_id=device, device_id_type=MESH)
    pl.semaphore_wait(barrier, len(devices))


def others(me, count):
    return [lax.rem(me + step, count) for step in range(1, count)]


def gather_kernel(cols, grad_ref, mask_ref, out_ref, send_sem, recv_sem):
    row, col = lax.axis_index("row"), lax.axis_index("col")
    out_ref[col] = (
        grad_ref[...].astype(jnp.float32) * mask_ref[...].astype(jnp.float32)
    ).astype(jnp.bfloat16)
    greet([(row, peer) for peer in others(col, cols)])
    sends = []
    for peer in others(col, cols):
        copy = remote(
            out_ref.at[col], out_ref.at[col], send_sem.at[peer], recv_sem.at[col], (row, peer)
        )
        copy.start()
        sends.append(copy)
    for peer in others(col, cols):
        remote(
            out_ref.at[peer], out_ref.at[peer], send_sem.at[peer], recv_sem.at[peer], (row, peer)
        ).wait_recv()
    for copy in sends:
        copy.wait_send()


def tiles_kernel(chunk, rows_ref, cols_ref, count_ref, masked_ref, vals_ref, out_ref, held, total, sems):
    slots, side = vals_ref.shape[0], vals_ref.shape[-1]
    columns = total.shape[0] - 1
    per_block = out_ref.shape[2] // side

    def fetch(index):
        part = pl.ds(index * chunk, chunk)
        return pltpu.make_async_copy(vals_ref.at[part], held.at[part], sems.at[index])

    for index in range(slots // chunk):
        fetch(index).start()
    total[...] = jnp.zeros_like(total)
    count = count_ref[0]

    @pl.loop(0, slots // chunk)
    def _(index):
        fetch(index).wait()

        @pl.when(index * chunk < count)
        def _():
            for step in range(chunk):
                tile = index * chunk + step
                start = pl.multiple_of(rows_ref[tile] * side, side)
                place = jnp.where(tile < count, cols_ref[tile], columns)
                total[place] += jnp.dot(
                    masked_ref[:, pl.ds(start, side)], held[tile], preferred_element_type=jnp.float32
                )

    for column in range(columns):
        block, part = divmod(column, per_block)
        out_ref[block, :, part * side : (part + 1) * side] = total[column].astype(jnp.bfloat16)


def reduce_kernel(
    outer,
    inner,
    cols,
    part_ref,
    feat_ref,
    weight_ref,
    imp_ref,
    delta_ref,
    grad_ref,
    imp_out_ref,
    pair_recv,
    pair_sum,
    line_recv,
    local_grad,
    col_recv,
    row_recv,
    whole_grad,
    pair_send_sem,
    pair_recv_sem,
    line_send_sem,
    line_recv_sem,
    col_send_sem,
    col_recv_sem,
    row_send_sem,
    row_recv_sem,
    all_send_sem,
    all_recv_sem,
):
    row, col = lax.axis_index("row"), lax.axis_index("col")
    rows = outer * inner
    my_outer, my_inner = lax.div(row, inner), lax.rem(row, inner)
    greet(
        [(peer, col) for peer in others(row, rows)] + [(row, peer) for peer in others(col, cols)]
    )
    sends = []

    def start(copy):
        copy.start()
        sends.append(copy)

    def arrived(slot, sem):
        remote(slot, slot, sem, sem, (row, col)).wait_recv()

    order = others(my_outer, outer) + [my_outer]
    for block in order:
        for peer in others(my_inner, inner):
            start(
                remote(
                    part_ref.at[block * inner + peer],
                    pair_recv.at[my_inner, block],
                    pair_send_sem.at[peer, block],
                    pair_recv_sem.at[my_inner, block],
                    (my_outer * inner + peer, col),
                )
            )
    value = None
    for block in order:
        value = part_ref[block * inner + my_inner].astype(jnp.float32)
        for peer in others(my_inner, inner):
            arrived(pair_recv.at[peer, block], pair_recv_sem.at[peer, block])
            value += pair_recv[peer, block].astype(jnp.float32)
        if block is not my_outer:
            pair_sum[block] = value.astype(jnp.bfloat16)
            start(
                remote(
                    pair_sum.at[block],
                    line_recv.at[my_outer],
                    line_send_sem.at[block],
                    line_recv_sem.at[my_outer],
                    (block * inner + my_inner, col),
                )
            )
    for peer in others(my_outer, outer):
        arrived(line_recv.at[peer], line_recv_sem.at[peer])
        value += line_recv[peer].astype(jnp.float32)
    aggregate = value.astype(jnp.bfloat16)

    local_grad[...] = jnp.dot(
        aggregate, feat_ref[...], preferred_element_type=jnp.float32
    ).T
    piece = local_grad.shape[0] // cols

    def rows_of(ref, index):
        return ref.at[pl.ds(pl.multiple_of(index * piece, piece), piece)]

    for peer in others(col, cols):
        start(
            remote(
                rows_of(local_grad, peer),
                col_recv.at[col],
                col_send_sem.at[peer],
                col_recv_sem.at[col],
                (row, peer),
            )
        )
    grad_ref[...] = (
        jnp.dot(weight_ref[...], aggregate, preferred_element_type=jnp.float32)
        .T.astype(jnp.bfloat16)
    )
    piece_sum = rows_of(local_grad, col)[...]
    for peer in others(col, cols):
        arrived(col_recv.at[peer], col_recv_sem.at[peer])
        piece_sum += col_recv[peer]
    row_recv[row] = piece_sum
    for peer in others(row, rows):
        start(
            remote(
                row_recv.at[row],
                row_recv.at[row],
                row_send_sem.at[peer],
                row_recv_sem.at[row],
                (peer, col),
            )
        )
    for peer in others(row, rows):
        arrived(row_recv.at[peer], row_recv_sem.at[peer])
    piece_sum = row_recv[0]
    for index in range(1, rows):
        piece_sum += row_recv[index]
    rows_of(whole_grad, col)[...] = piece_sum
    for peer in others(col, cols):
        start(
            remote(
                rows_of(whole_grad, col),
                rows_of(whole_grad, col),
                all_send_sem.at[peer],
                all_recv_sem.at[col],
                (row, peer),
            )
        )
    for peer in others(col, cols):
        arrived(rows_of(whole_grad, peer), all_recv_sem.at[peer])
    imp_out_ref[...] = imp_ref[...] - whole_grad[...] * delta_ref[...]
    for copy in sends:
        copy.wait_send()


def local(
    rows,
    cols,
    tile_vals,
    tile_row,
    tile_col,
    tile_count,
    out_grad,
    relu_mask,
    features,
    weight,
    importance,
    weight_delta,
):
    slots, side = tile_vals.shape[2], tile_vals.shape[-1]
    nodes, depth = features.shape
    block_nodes, own_width = out_grad.shape
    width = own_width * cols
    columns = rows * nodes // side
    inner = 2 if rows % 2 == 0 else 1
    outer = rows // inner
    chunk = 16
    params = functools.partial(pltpu.CompilerParams, vmem_limit_bytes=48 * 2**20)
    dma = pltpu.SemaphoreType.DMA

    masked = pl.pallas_call(
        functools.partial(gather_kernel, cols),
        out_shape=jax.ShapeDtypeStruct((cols, own_width, block_nodes), jnp.bfloat16),
        in_specs=[VMEM] * 2,
        out_specs=VMEM,
        scratch_shapes=[dma((cols,)), dma((cols,))],
        compiler_params=params(collective_id=0, has_side_effects=True),
        name="gather_masked",
    )(out_grad.T, relu_mask.T)

    partial_value = pl.pallas_call(
        functools.partial(tiles_kernel, chunk),
        out_shape=jax.ShapeDtypeStruct((rows, width, nodes), jnp.bfloat16),
        in_specs=[SMEM, SMEM, SMEM, VMEM, pl.BlockSpec(memory_space=pl.ANY)],
        out_specs=VMEM,
        scratch_shapes=[
            pltpu.VMEM((slots, side, side), jnp.bfloat16),
            pltpu.VMEM((columns + 1, width, side), jnp.float32),
            dma((slots // chunk,)),
        ],
        compiler_params=params(),
        name="tile_products",
    )(
        tile_row.reshape(slots),
        tile_col.reshape(slots),
        tile_count.reshape(1),
        masked.reshape(width, block_nodes),
        tile_vals.reshape(slots, side, side),
    )

    piece = depth // cols
    return pl.pallas_call(
        functools.partial(reduce_kernel, outer, inner, cols),
        out_shape=(
            jax.ShapeDtypeStruct((nodes, depth), jnp.bfloat16),
            jax.ShapeDtypeStruct((depth, width), jnp.float32),
        ),
        in_specs=[VMEM] * 5,
        out_specs=(VMEM, VMEM),
        scratch_shapes=[
            pltpu.VMEM((inner, outer, width, nodes), jnp.bfloat16),
            pltpu.VMEM((outer, width, nodes), jnp.bfloat16),
            pltpu.VMEM((outer, width, nodes), jnp.bfloat16),
            pltpu.VMEM((depth, width), jnp.float32),
            pltpu.VMEM((cols, piece, width), jnp.float32),
            pltpu.VMEM((rows, piece, width), jnp.float32),
            pltpu.VMEM((depth, width), jnp.float32),
            dma((inner, outer)),
            dma((inner, outer)),
            dma((outer,)),
            dma((outer,)),
            dma((cols,)),
            dma((cols,)),
            dma((rows,)),
            dma((rows,)),
            dma((cols,)),
            dma((cols,)),
        ],
        compiler_params=params(collective_id=1, has_side_effects=True),
        name="reduce_and_update",
    )(partial_value, features, weight, importance, weight_delta)


def solution(mesh):
    return jax.shard_map(
        functools.partial(local, mesh.shape["row"], mesh.shape["col"]),
        mesh=mesh,
        in_specs=(
            P("row", "col", None, None, None),
            P("row", "col", None),
            P("row", "col", None),
            P("row", "col"),
            P("row", "col"),
            P("row", "col"),
            P(("row", "col"), None),
            P(),
            P(),
            P(),
        ),
        out_specs=(P(("row", "col"), None), P()),
        check_vma=False,
    )
```

```python
import functools

import jax
import jax.numpy as jnp
from jax import lax
from jax.experimental import pallas as pl
from jax.experimental.pallas import tpu as pltpu
from jax.sharding import PartitionSpec as P

MESH = pl.DeviceIdType.MESH
SMEM = pl.BlockSpec(memory_space=pltpu.SMEM)
HBM = pl.BlockSpec(memory_space=pltpu.HBM)


def remote(src, dst, send_sem, recv_sem, device):
    return pltpu.make_async_remote_copy(
        src_ref=src,
        dst_ref=dst,
        send_sem=send_sem,
        recv_sem=recv_sem,
        device_id=device,
        device_id_type=MESH,
    )


def greet(devices):
    barrier = pltpu.get_barrier_semaphore()
    for device in devices:
        pl.semaphore_signal(barrier, inc=1, device_id=device, device_id_type=MESH)
    pl.semaphore_wait(barrier, len(devices))


def others(me, count):
    return [lax.rem(me + step, count) for step in range(1, count)]


def mate_of(index):
    return index + 1 - 2 * lax.rem(index, 2)


def gather_kernel(
    cols,
    parts,
    grad_hbm,
    mask_hbm,
    out_ref,
    grad_ref,
    mask_ref,
    own_ref,
    load_sem,
    store_sem,
    send_sem,
    pass_sem,
    recv_sem,
):
    row, col = lax.axis_index("row"), lax.axis_index("col")
    loads = [
        pltpu.make_async_copy(grad_hbm, grad_ref, load_sem.at[0]),
        pltpu.make_async_copy(mask_hbm, mask_ref, load_sem.at[1]),
    ]
    for load in loads:
        load.start()
    mate = mate_of(col)
    far = [lax.rem(col + 2 * step, cols) for step in range(1, cols // 2)]
    greet([(row, peer) for peer in [mate] + far])
    for load in loads:
        load.wait()
    size = out_ref.shape[2] // parts
    sends = []

    def piece(block, part):
        return out_ref.at[block, :, part * size : (part + 1) * size]

    def send(part, peer):
        copy = remote(
            own_ref.at[:, part * size : (part + 1) * size],
            piece(col, part),
            send_sem.at[peer, part],
            recv_sem.at[col, part],
            (row, peer),
        )
        copy.start()
        sends.append(copy)

    def arrived(block, part):
        ref = piece(block, part)
        sem = recv_sem.at[block, part]
        remote(ref, ref, sem, sem, (row, mate)).wait_recv()

    for part in range(parts):
        lanes = slice(part * size, (part + 1) * size)
        own_ref[:, lanes] = (
            grad_ref[:, lanes].astype(jnp.float32) * mask_ref[:, lanes].astype(jnp.float32)
        ).astype(jnp.bfloat16)
        for peer in far:
            send(part, peer)
    for part in range(parts):
        send(part, mate)
    store = pltpu.make_async_copy(own_ref, out_ref.at[col], store_sem.at[0])
    store.start()
    for part in range(parts):
        for peer in far:
            arrived(peer, part)
            ref = piece(peer, part)
            copy = remote(
                ref, ref, pass_sem.at[peer, part], recv_sem.at[peer, part], (row, mate)
            )
            copy.start()
            sends.append(copy)
    for part in range(parts):
        arrived(mate, part)
    for part in range(parts):
        for peer in far:
            arrived(mate_of(peer), part)
    store.wait()
    for copy in sends:
        copy.wait_send()


def tiles_kernel(
    chunk,
    rows_hbm,
    cols_hbm,
    count_ref,
    masked_hbm,
    vals_ref,
    out_hbm,
    held,
    total,
    rows_ref,
    cols_ref,
    masked_ref,
    out_ref,
    sems,
    load_sem,
    store_sem,
):
    slots, side = vals_ref.shape[0], vals_ref.shape[-1]
    columns = total.shape[0] - 1
    per_block = out_ref.shape[2] // side

    def fetch(index):
        part = pl.ds(index * chunk, chunk)
        return pltpu.make_async_copy(vals_ref.at[part], held.at[part], sems.at[index])

    loads = [
        pltpu.make_async_copy(rows_hbm, rows_ref, load_sem.at[0]),
        pltpu.make_async_copy(cols_hbm, cols_ref, load_sem.at[1]),
        pltpu.make_async_copy(masked_hbm, masked_ref, load_sem.at[2]),
    ]
    for load in loads:
        load.start()
    for index in range(slots // chunk):
        fetch(index).start()
    total[...] = jnp.zeros_like(total)
    for load in loads:
        load.wait()
    count = count_ref[0, 0]

    @pl.loop(0, slots // chunk)
    def _(index):
        fetch(index).wait()

        @pl.when(index * chunk < count)
        def _():
            for step in range(chunk):
                tile = index * chunk + step
                start = pl.multiple_of(rows_ref[0, tile] * side, side)
                place = jnp.where(tile < count, cols_ref[0, tile], columns)
                total[place] += jnp.dot(
                    masked_ref[:, pl.ds(start, side)], held[tile], preferred_element_type=jnp.float32
                )

    stores = []
    for column in range(columns):
        block, part = divmod(column, per_block)
        out_ref[block, :, part * side : (part + 1) * side] = total[column].astype(jnp.bfloat16)
        if part == per_block - 1:
            store = pltpu.make_async_copy(out_ref.at[block], out_hbm.at[block], store_sem.at[block])
            store.start()
            stores.append(store)
    for store in stores:
        store.wait()


def reduce_kernel(
    outer,
    inner,
    cols,
    part_hbm,
    feat_hbm,
    weight_hbm,
    imp_hbm,
    delta_hbm,
    grad_hbm,
    imp_out_hbm,
    part_ref,
    feat_ref,
    weight_ref,
    imp_ref,
    delta_ref,
    grad_ref,
    imp_out_ref,
    load_sem,
    part_sem,
    store_sem,
    pair_recv,
    pair_sum,
    line_recv,
    local_grad,
    col_recv,
    row_recv,
    whole_grad,
    pair_send_sem,
    pair_recv_sem,
    line_send_sem,
    line_recv_sem,
    col_send_sem,
    col_recv_sem,
    row_send_sem,
    row_recv_sem,
    all_send_sem,
    all_recv_sem,
):
    row, col = lax.axis_index("row"), lax.axis_index("col")
    rows = outer * inner
    my_outer, my_inner = lax.div(row, inner), lax.rem(row, inner)
    part_loads = [
        pltpu.make_async_copy(
            part_hbm.at[block * inner + my_inner], part_ref.at[block], part_sem.at[block]
        )
        for block in range(outer)
    ]
    loads = [
        pltpu.make_async_copy(source, target, load_sem.at[index])
        for index, (source, target) in enumerate(
            [(feat_hbm, feat_ref), (weight_hbm, weight_ref), (imp_hbm, imp_ref), (delta_hbm, delta_ref)]
        )
    ]
    for load in part_loads + loads:
        load.start()
    greet(
        [(peer, col) for peer in others(row, rows)] + [(row, peer) for peer in others(col, cols)]
    )
    sends = []

    def start(copy):
        copy.start()
        sends.append(copy)

    def arrived(slot, sem):
        remote(slot, slot, sem, sem, (row, col)).wait_recv()

    if outer == 4:
        across = lax.rem(my_outer + 2, outer)
        order = [across, mate_of(across), mate_of(my_outer), my_outer]
    else:
        order = others(my_outer, outer) + [my_outer]
    halves = 2
    height = part_ref.shape[1] // halves
    steps = [(block, half) for block in order for half in range(halves)]

    def strip(half):
        return pl.ds(half * height, height)

    def pair_sends(step):
        block, half = steps[step]
        return [
            remote(
                part_hbm.at[block * inner + peer, strip(half)],
                pair_recv.at[my_inner, block, strip(half)],
                pair_send_sem.at[peer, block, half],
                pair_recv_sem.at[my_inner, block, half],
                (my_outer * inner + peer, col),
            )
            for peer in others(my_inner, inner)
        ]

    for step in range(2):
        for copy in pair_sends(step):
            copy.start()
    for load in part_loads + loads:
        load.wait()
    values = []
    for step, (block, half) in enumerate(steps):
        for copy in pair_sends(step):
            copy.wait_send()
        if step + 2 < len(steps):
            for copy in pair_sends(step + 2):
                copy.start()
        value = part_ref[block, strip(half)].astype(jnp.float32)
        for peer in others(my_inner, inner):
            arrived(pair_recv.at[peer, block, strip(half)], pair_recv_sem.at[peer, block, half])
            value += pair_recv[peer, block, strip(half)].astype(jnp.float32)
        if block is my_outer:
            values.append(value)
        else:
            pair_sum[block, strip(half)] = value.astype(jnp.bfloat16)
            start(
                remote(
                    pair_sum.at[block, strip(half)],
                    line_recv.at[my_outer, strip(half)],
                    line_send_sem.at[block, half],
                    line_recv_sem.at[my_outer, half],
                    (block * inner + my_inner, col),
                )
            )
    for half in range(halves):
        for peer in reversed(order[:-1]):
            arrived(line_recv.at[peer, strip(half)], line_recv_sem.at[peer, half])
            values[half] += line_recv[peer, strip(half)].astype(jnp.float32)
    aggregate = jnp.concatenate(values, axis=0).astype(jnp.bfloat16)

    local_grad[...] = jnp.dot(
        aggregate, feat_ref[...], preferred_element_type=jnp.float32
    ).T
    piece = local_grad.shape[0] // cols

    def rows_of(ref, index):
        return ref.at[pl.ds(pl.multiple_of(index * piece, piece), piece)]

    for peer in others(col, cols):
        start(
            remote(
                rows_of(local_grad, peer),
                col_recv.at[col],
                col_send_sem.at[peer],
                col_recv_sem.at[col],
                (row, peer),
            )
        )
    grad_ref[...] = (
        jnp.dot(weight_ref[...], aggregate, preferred_element_type=jnp.float32)
        .T.astype(jnp.bfloat16)
    )
    grad_store = pltpu.make_async_copy(grad_ref, grad_hbm, store_sem.at[0])
    grad_store.start()
    piece_sum = rows_of(local_grad, col)[...]
    for peer in others(col, cols):
        arrived(col_recv.at[peer], col_recv_sem.at[peer])
        piece_sum += col_recv[peer]
    row_recv[row] = piece_sum
    for peer in others(row, rows):
        start(
            remote(
                row_recv.at[row],
                row_recv.at[row],
                row_send_sem.at[peer],
                row_recv_sem.at[row],
                (peer, col),
            )
        )
    for peer in others(row, rows):
        arrived(row_recv.at[peer], row_recv_sem.at[peer])
    piece_sum = row_recv[0]
    for index in range(1, rows):
        piece_sum += row_recv[index]
    rows_of(whole_grad, col)[...] = piece_sum
    for peer in others(col, cols):
        start(
            remote(
                rows_of(whole_grad, col),
                rows_of(whole_grad, col),
                all_send_sem.at[peer],
                all_recv_sem.at[col],
                (row, peer),
            )
        )
    for peer in others(col, cols):
        arrived(rows_of(whole_grad, peer), all_recv_sem.at[peer])
    imp_out_ref[...] = imp_ref[...] - whole_grad[...] * delta_ref[...]
    imp_store = pltpu.make_async_copy(imp_out_ref, imp_out_hbm, store_sem.at[1])
    imp_store.start()
    for copy in sends:
        copy.wait_send()
    grad_store.wait()
    imp_store.wait()


def local(
    rows,
    cols,
    tile_vals,
    tile_row,
    tile_col,
    tile_count,
    out_grad,
    relu_mask,
    features,
    weight,
    importance,
    weight_delta,
):
    slots, side = tile_vals.shape[2], tile_vals.shape[-1]
    nodes, depth = features.shape
    block_nodes, own_width = out_grad.shape
    width = own_width * cols
    columns = rows * nodes // side
    inner = 2 if rows % 2 == 0 else 1
    outer = rows // inner
    chunk = 16
    params = functools.partial(pltpu.CompilerParams, vmem_limit_bytes=60 * 2**20)
    dma = pltpu.SemaphoreType.DMA

    masked = pl.pallas_call(
        functools.partial(gather_kernel, cols, 4),
        out_shape=jax.ShapeDtypeStruct((cols, own_width, block_nodes), jnp.bfloat16),
        in_specs=[HBM] * 2,
        out_specs=HBM,
        scratch_shapes=[
            pltpu.VMEM((own_width, block_nodes), jnp.bfloat16),
            pltpu.VMEM((own_width, block_nodes), jnp.int32),
            pltpu.VMEM((own_width, block_nodes), jnp.bfloat16),
            dma((2,)),
            dma((1,)),
            dma((cols, 4)),
            dma((cols, 4)),
            dma((cols, 4)),
        ],
        compiler_params=params(collective_id=0, has_side_effects=True),
        name="gather_masked",
    )(out_grad.T, relu_mask.T)

    partial_value = pl.pallas_call(
        functools.partial(tiles_kernel, chunk),
        out_shape=jax.ShapeDtypeStruct((rows, width, nodes), jnp.bfloat16),
        in_specs=[HBM, HBM, SMEM, HBM, HBM],
        out_specs=HBM,
        scratch_shapes=[
            pltpu.VMEM((slots, side, side), jnp.bfloat16),
            pltpu.VMEM((columns + 1, width, side), jnp.float32),
            pltpu.SMEM((1, slots), jnp.int32),
            pltpu.SMEM((1, slots), jnp.int32),
            pltpu.VMEM((width, block_nodes), jnp.bfloat16),
            pltpu.VMEM((rows, width, nodes), jnp.bfloat16),
            dma((slots // chunk,)),
            dma((3,)),
            dma((rows,)),
        ],
        compiler_params=params(),
        name="tile_products",
    )(
        tile_row.reshape(1, slots),
        tile_col.reshape(1, slots),
        tile_count,
        masked.reshape(width, block_nodes),
        tile_vals.reshape(slots, side, side),
    )

    piece = depth // cols
    return pl.pallas_call(
        functools.partial(reduce_kernel, outer, inner, cols),
        out_shape=(
            jax.ShapeDtypeStruct((nodes, depth), jnp.bfloat16),
            jax.ShapeDtypeStruct((depth, width), jnp.float32),
        ),
        in_specs=[HBM] * 5,
        out_specs=(HBM, HBM),
        scratch_shapes=[
            pltpu.VMEM((outer, width, nodes), jnp.bfloat16),
            pltpu.VMEM((nodes, depth), jnp.bfloat16),
            pltpu.VMEM((depth, width), jnp.bfloat16),
            pltpu.VMEM((depth, width), jnp.float32),
            pltpu.VMEM((depth, width), jnp.float32),
            pltpu.VMEM((nodes, depth), jnp.bfloat16),
            pltpu.VMEM((depth, width), jnp.float32),
            dma((4,)),
            dma((outer,)),
            dma((2,)),
            pltpu.VMEM((inner, outer, width, nodes), jnp.bfloat16),
            pltpu.VMEM((outer, width, nodes), jnp.bfloat16),
            pltpu.VMEM((outer, width, nodes), jnp.bfloat16),
            pltpu.VMEM((depth, width), jnp.float32),
            pltpu.VMEM((cols, piece, width), jnp.float32),
            pltpu.VMEM((rows, piece, width), jnp.float32),
            pltpu.VMEM((depth, width), jnp.float32),
            dma((inner, outer, 2)),
            dma((inner, outer, 2)),
            dma((outer, 2)),
            dma((outer, 2)),
            dma((cols,)),
            dma((cols,)),
            dma((rows,)),
            dma((rows,)),
            dma((cols,)),
            dma((cols,)),
        ],
        compiler_params=params(collective_id=1, has_side_effects=True),
        name="reduce_and_update",
    )(partial_value, features, weight, importance, weight_delta)


def solution(mesh):
    return jax.shard_map(
        functools.partial(local, mesh.shape["row"], mesh.shape["col"]),
        mesh=mesh,
        in_specs=(
            P("row", "col", None, None, None),
            P("row", "col", None),
            P("row", "col", None),
            P("row", "col"),
            P("row", "col"),
            P("row", "col"),
            P(("row", "col"), None),
            P(),
            P(),
            P(),
        ),
        out_specs=(P(("row", "col"), None), P()),
        check_vma=False,
    )
```

```python
import functools

import jax
import jax.numpy as jnp
from jax import lax
from jax.experimental import pallas as pl
from jax.experimental.pallas import tpu as pltpu
from jax.sharding import PartitionSpec as P

MESH = pl.DeviceIdType.MESH
SMEM = pl.BlockSpec(memory_space=pltpu.SMEM)
HBM = pl.BlockSpec(memory_space=pltpu.HBM)
PARTS = 4
HALVES = 2
CHUNK = 16


def remote(src, dst, send_sem, recv_sem, device):
    return pltpu.make_async_remote_copy(
        src_ref=src,
        dst_ref=dst,
        send_sem=send_sem,
        recv_sem=recv_sem,
        device_id=device,
        device_id_type=MESH,
    )


def greet(devices):
    barrier = pltpu.get_barrier_semaphore()
    for device in devices:
        pl.semaphore_signal(barrier, inc=1, device_id=device, device_id_type=MESH)
    pl.semaphore_wait(barrier, len(devices))


def others(me, count):
    return [lax.rem(me + step, count) for step in range(1, count)]


def mate_of(index):
    return index + 1 - 2 * lax.rem(index, 2)


def sort_tables(cols, rows, count, columns):
    slots = cols.shape[1]
    shape = (slots, slots)
    lane = lax.broadcasted_iota(jnp.int32, shape, 1)
    sublane = lax.broadcasted_iota(jnp.int32, shape, 0)
    diagonal = lane == sublane
    here = jnp.broadcast_to(cols, shape)
    key = jnp.where(lane < count, here, columns)

    def upright(value):
        return jnp.sum(jnp.where(diagonal, value, 0), axis=1, keepdims=True)

    mine = upright(key)
    row = upright(jnp.broadcast_to(rows, shape))
    earlier = (key == mine) & (lane < sublane)
    rank = jnp.sum(jnp.where((key < mine) | earlier, 1, 0), axis=1, keepdims=True)
    keep = jnp.max(jnp.where(earlier, 1, 0), axis=1, keepdims=True)
    placed = rank == lane

    def in_order(value):
        return jnp.sum(jnp.where(placed, value, 0), axis=0, keepdims=True)

    first = jnp.sum(jnp.where(mine < lane, 1, 0), axis=0, keepdims=True)
    last = jnp.sum(jnp.where(mine <= lane, 1, 0), axis=0, keepdims=True)
    return in_order(sublane), in_order(row), in_order(keep), first, last


def layer_kernel(
    outer,
    inner,
    cols,
    rows_hbm,
    cols_hbm,
    count_ref,
    grad_hbm,
    mask_hbm,
    vals_hbm,
    feat_hbm,
    weight_hbm,
    node_out_hbm,
    weight_out_hbm,
    grad_ref,
    mask_ref,
    masked_ref,
    held,
    tile_rows_ref,
    tile_cols_ref,
    table_ref,
    table,
    sums,
    part_ref,
    feat_ref,
    weight_ref,
    node_out_ref,
    pair_recv,
    pair_sum,
    line_recv,
    local_grad,
    col_recv,
    row_recv,
    whole_grad,
    load_sem,
    tile_sem,
    table_sem,
    store_sem,
    send_sem,
    pass_sem,
    recv_sem,
    pair_send_sem,
    pair_recv_sem,
    line_send_sem,
    line_recv_sem,
    col_send_sem,
    col_recv_sem,
    row_send_sem,
    row_recv_sem,
    all_send_sem,
    all_recv_sem,
):
    row, col = lax.axis_index("row"), lax.axis_index("col")
    rows = outer * inner
    my_outer, my_inner = lax.div(row, inner), lax.rem(row, inner)
    slots, side = held.shape[0], held.shape[-1]
    width, nodes = part_ref.shape[1:]
    per_block = nodes // side
    columns = rows * per_block
    sends = []

    def start(copy):
        copy.start()
        sends.append(copy)

    def arrived(slot, sem):
        remote(slot, slot, sem, sem, (row, mate_of(col))).wait_recv()

    loads = [
        pltpu.make_async_copy(source, target, load_sem.at[index])
        for index, (source, target) in enumerate(
            [
                (grad_hbm, grad_ref),
                (mask_hbm, mask_ref),
                (rows_hbm, tile_rows_ref),
                (cols_hbm, tile_cols_ref),
                (feat_hbm, feat_ref),
                (weight_hbm, weight_ref),
            ]
        )
    ]
    for load in loads:
        load.start()
    tile_loads = []
    for index in range(slots // CHUNK):
        piece = pl.ds(index * CHUNK, CHUNK)
        load = pltpu.make_async_copy(vals_hbm.at[piece], held.at[piece], tile_sem.at[index])
        load.start()
        tile_loads.append(load)
    greet(
        [(row, peer) for peer in others(col, cols)] + [(peer, col) for peer in others(row, rows)]
    )

    loads[0].wait()
    loads[1].wait()
    mate = mate_of(col)
    far = [lax.rem(col + 2 * step, cols) for step in range(1, cols // 2)]
    row_tiles = masked_ref.shape[0]
    size = row_tiles // PARTS
    own_width = grad_ref.shape[0]

    def masked_piece(block, part):
        lines = pl.ds(pl.multiple_of(block * own_width, own_width), own_width)
        return masked_ref.at[part * size : (part + 1) * size, lines]

    def send_masked(block, part, sems, peer):
        ref = masked_piece(block, part)
        start(remote(ref, ref, sems.at[peer, part], recv_sem.at[block, part], (row, peer)))

    def masked_arrived(block, part):
        arrived(masked_piece(block, part), recv_sem.at[block, part])

    for part in range(PARTS):
        for tile in range(part * size, (part + 1) * size):
            lanes = slice(tile * side, (tile + 1) * side)
            lines = pl.ds(pl.multiple_of(col * own_width, own_width), own_width)
            masked_ref[tile, lines, :] = (
                grad_ref[:, lanes].astype(jnp.float32) * mask_ref[:, lanes].astype(jnp.float32)
            ).astype(jnp.bfloat16)
        for peer in far:
            send_masked(col, part, send_sem, peer)
    for part in range(PARTS):
        send_masked(col, part, send_sem, mate)
    loads[2].wait()
    loads[3].wait()
    for index, line in enumerate(
        sort_tables(tile_cols_ref[...], tile_rows_ref[...], count_ref[0, 0], columns)
    ):
        table_ref[index : index + 1, :] = line
    to_scalars = pltpu.make_async_copy(table_ref, table, table_sem.at[0])
    to_scalars.start()
    for part in range(PARTS):
        for peer in far:
            masked_arrived(peer, part)
            send_masked(peer, part, pass_sem, mate)
    to_scalars.wait()
    for load in tile_loads + loads[4:]:
        load.wait()
    for part in range(PARTS):
        masked_arrived(mate, part)
        for peer in far:
            masked_arrived(mate_of(peer), part)

    def chunk_step(index, running):
        for step in range(CHUNK):
            place = index * CHUNK + step
            product = jnp.dot(
                masked_ref[table[1, place]],
                held[table[0, place]],
                preferred_element_type=jnp.float32,
            )
            running = running * table[2, place].astype(jnp.float32) + product
            sums[place] = running.astype(jnp.bfloat16)
        return running

    lax.fori_loop(0, slots // CHUNK, chunk_step, jnp.zeros((width, side), jnp.float32))

    def pack(block):
        for part in range(per_block):
            column = block * per_block + part
            begin, end = table[3, column], table[4, column]
            used = jnp.minimum(end - begin, 1).astype(jnp.float32)
            value = sums[jnp.maximum(end - 1, 0)].astype(jnp.float32) * used
            part_ref[block, :, part * side : (part + 1) * side] = value.astype(jnp.bfloat16)

    if outer == 4:
        across = lax.rem(my_outer + 2, outer)
        order = [across, mate_of(across), mate_of(my_outer), my_outer]
    else:
        order = others(my_outer, outer) + [my_outer]
    height = width // HALVES
    steps = [(block, half) for block in order for half in range(HALVES)]

    def strip(half):
        return pl.ds(half * height, height)

    def pair_sends(step):
        block, half = steps[step]
        return [
            remote(
                part_ref.at[block * inner + peer, strip(half)],
                pair_recv.at[my_inner, block, strip(half)],
                pair_send_sem.at[peer, block, half],
                pair_recv_sem.at[my_inner, block, half],
                (my_outer * inner + peer, col),
            )
            for peer in others(my_inner, inner)
        ]

    for index, block in enumerate(order):
        for peer in others(my_inner, inner):
            pack(block * inner + peer)
        if index == 0:
            for step in range(2):
                for copy in pair_sends(step):
                    copy.start()
    for block in order:
        pack(block * inner + my_inner)
    values = []
    for step, (block, half) in enumerate(steps):
        for copy in pair_sends(step):
            copy.wait_send()
        if step + 2 < len(steps):
            for copy in pair_sends(step + 2):
                copy.start()
        value = part_ref[block * inner + my_inner, strip(half)].astype(jnp.float32)
        for peer in others(my_inner, inner):
            arrived(pair_recv.at[peer, block, strip(half)], pair_recv_sem.at[peer, block, half])
            value += pair_recv[peer, block, strip(half)].astype(jnp.float32)
        if block is my_outer:
            values.append(value)
        else:
            pair_sum[block, strip(half)] = value.astype(jnp.bfloat16)
            start(
                remote(
                    pair_sum.at[block, strip(half)],
                    line_recv.at[my_outer, strip(half)],
                    line_send_sem.at[block, half],
                    line_recv_sem.at[my_outer, half],
                    (block * inner + my_inner, col),
                )
            )
    for half in range(HALVES):
        for peer in reversed(order[:-1]):
            arrived(line_recv.at[peer, strip(half)], line_recv_sem.at[peer, half])
            values[half] += line_recv[peer, strip(half)].astype(jnp.float32)
    aggregate = jnp.concatenate(values, axis=0).astype(jnp.bfloat16)

    local_grad[...] = jnp.dot(
        aggregate, feat_ref[...], preferred_element_type=jnp.float32
    ).T
    piece = local_grad.shape[0] // cols

    def rows_of(ref, index):
        return ref.at[pl.ds(pl.multiple_of(index * piece, piece), piece)]

    for peer in others(col, cols):
        start(
            remote(
                rows_of(local_grad, peer),
                col_recv.at[col],
                col_send_sem.at[peer],
                col_recv_sem.at[col],
                (row, peer),
            )
        )
    node_out_ref[...] = (
        jnp.dot(weight_ref[...], aggregate, preferred_element_type=jnp.float32)
        .T.astype(jnp.bfloat16)
    )
    node_store = pltpu.make_async_copy(node_out_ref, node_out_hbm, store_sem.at[0])
    node_store.start()
    piece_sum = rows_of(local_grad, col)[...]
    for peer in others(col, cols):
        arrived(col_recv.at[peer], col_recv_sem.at[peer])
        piece_sum += col_recv[peer]
    row_recv[row] = piece_sum
    for peer in others(row, rows):
        start(
            remote(
                row_recv.at[row],
                row_recv.at[row],
                row_send_sem.at[peer],
                row_recv_sem.at[row],
                (peer, col),
            )
        )
    for peer in others(row, rows):
        arrived(row_recv.at[peer], row_recv_sem.at[peer])
    piece_sum = row_recv[0]
    for index in range(1, rows):
        piece_sum += row_recv[index]
    rows_of(whole_grad, col)[...] = piece_sum
    for peer in others(col, cols):
        start(
            remote(
                rows_of(whole_grad, col),
                rows_of(whole_grad, col),
                all_send_sem.at[peer],
                all_recv_sem.at[col],
                (row, peer),
            )
        )
    for peer in others(col, cols):
        arrived(rows_of(whole_grad, peer), all_recv_sem.at[peer])
    weight_store = pltpu.make_async_copy(whole_grad, weight_out_hbm, store_sem.at[1])
    weight_store.start()
    for copy in sends:
        copy.wait_send()
    node_store.wait()
    weight_store.wait()


def finish_kernel(
    node_hbm, grad_hbm, imp_hbm, delta_hbm, node_out, imp_out, node_ref, grad_ref, imp_ref, delta_ref, sems
):
    loads = [
        pltpu.make_async_copy(source, target, sems.at[index])
        for index, (source, target) in enumerate(
            [(node_hbm, node_ref), (grad_hbm, grad_ref), (imp_hbm, imp_ref), (delta_hbm, delta_ref)]
        )
    ]
    for load in loads:
        load.start()
    loads[0].wait()
    node_store = pltpu.make_async_copy(node_ref, node_out, sems.at[4])
    node_store.start()
    for load in loads[1:]:
        load.wait()
    imp_ref[...] = imp_ref[...] - grad_ref[...] * delta_ref[...]
    imp_store = pltpu.make_async_copy(imp_ref, imp_out, sems.at[5])
    imp_store.start()
    node_store.wait()
    imp_store.wait()


def local(
    rows,
    cols,
    tile_vals,
    tile_row,
    tile_col,
    tile_count,
    out_grad,
    relu_mask,
    features,
    weight,
    importance,
    weight_delta,
):
    slots, side = tile_vals.shape[2], tile_vals.shape[-1]
    nodes, depth = features.shape
    block_nodes, own_width = out_grad.shape
    width = own_width * cols
    inner = 2 if rows % 2 == 0 else 1
    outer = rows // inner
    params = functools.partial(pltpu.CompilerParams, vmem_limit_bytes=60 * 2**20)
    dma = pltpu.SemaphoreType.DMA
    piece = depth // cols
    bf16 = jnp.bfloat16
    f32 = jnp.float32
    i32 = jnp.int32

    node_grad, weight_grad = pl.pallas_call(
        functools.partial(layer_kernel, outer, inner, cols),
        out_shape=(
            jax.ShapeDtypeStruct((nodes, depth), bf16),
            jax.ShapeDtypeStruct((depth, width), f32),
        ),
        in_specs=[HBM, HBM, SMEM] + [HBM] * 5,
        out_specs=(HBM, HBM),
        scratch_shapes=[
            pltpu.VMEM((own_width, block_nodes), bf16),
            pltpu.VMEM((own_width, block_nodes), i32),
            pltpu.VMEM((block_nodes // side, width, side), bf16),
            pltpu.VMEM((slots, side, side), bf16),
            pltpu.VMEM((1, slots), i32),
            pltpu.VMEM((1, slots), i32),
            pltpu.VMEM((8, slots), i32),
            pltpu.SMEM((8, slots), i32),
            pltpu.VMEM((slots, width, side), bf16),
            pltpu.VMEM((rows, width, nodes), bf16),
            pltpu.VMEM((nodes, depth), bf16),
            pltpu.VMEM((depth, width), bf16),
            pltpu.VMEM((nodes, depth), bf16),
            pltpu.VMEM((inner, outer, width, nodes), bf16),
            pltpu.VMEM((outer, width, nodes), bf16),
            pltpu.VMEM((outer, width, nodes), bf16),
            pltpu.VMEM((depth, width), f32),
            pltpu.VMEM((cols, piece, width), f32),
            pltpu.VMEM((rows, piece, width), f32),
            pltpu.VMEM((depth, width), f32),
            dma((6,)),
            dma((slots // CHUNK,)),
            dma((1,)),
            dma((2,)),
            dma((cols, PARTS)),
            dma((cols, PARTS)),
            dma((cols, PARTS)),
            dma((inner, outer, HALVES)),
            dma((inner, outer, HALVES)),
            dma((outer, HALVES)),
            dma((outer, HALVES)),
            dma((cols,)),
            dma((cols,)),
            dma((rows,)),
            dma((rows,)),
            dma((cols,)),
            dma((cols,)),
        ],
        compiler_params=params(collective_id=0, has_side_effects=True),
        name="layer_backward",
    )(
        tile_row.reshape(1, slots),
        tile_col.reshape(1, slots),
        tile_count,
        out_grad.T,
        relu_mask.T,
        tile_vals.reshape(slots, side, side),
        features,
        weight,
    )

    return pl.pallas_call(
        finish_kernel,
        out_shape=(
            jax.ShapeDtypeStruct((nodes, depth), bf16),
            jax.ShapeDtypeStruct((depth, width), f32),
        ),
        in_specs=[HBM] * 4,
        out_specs=(HBM, HBM),
        scratch_shapes=[
            pltpu.VMEM((nodes, depth), bf16),
            pltpu.VMEM((depth, width), f32),
            pltpu.VMEM((depth, width), f32),
            pltpu.VMEM((depth, width), f32),
            dma((6,)),
        ],
        compiler_params=params(),
        name="finish",
    )(node_grad, weight_grad, importance, weight_delta)


def solution(mesh):
    return jax.shard_map(
        functools.partial(local, mesh.shape["row"], mesh.shape["col"]),
        mesh=mesh,
        in_specs=(
            P("row", "col", None, None, None),
            P("row", "col", None),
            P("row", "col", None),
            P("row", "col"),
            P("row", "col"),
            P("row", "col"),
            P(("row", "col"), None),
            P(),
            P(),
            P(),
        ),
        out_specs=(P(("row", "col"), None), P()),
        check_vma=False,
    )
```

```python
import functools

import jax
import jax.numpy as jnp
from jax import lax
from jax.experimental import pallas as pl
from jax.experimental.pallas import tpu as pltpu
from jax.sharding import PartitionSpec as P

MESH = pl.DeviceIdType.MESH
SMEM = pl.BlockSpec(memory_space=pltpu.SMEM)
HBM = pl.BlockSpec(memory_space=pltpu.HBM)
PARTS = 4
HALVES = 2
CHUNK = 16


def remote(src, dst, send_sem, recv_sem, device):
    return pltpu.make_async_remote_copy(
        src_ref=src,
        dst_ref=dst,
        send_sem=send_sem,
        recv_sem=recv_sem,
        device_id=device,
        device_id_type=MESH,
    )


def greet(devices):
    barrier = pltpu.get_barrier_semaphore()
    for device in devices:
        pl.semaphore_signal(barrier, inc=1, device_id=device, device_id_type=MESH)
    pl.semaphore_wait(barrier, len(devices))


def others(me, count):
    return [lax.rem(me + step, count) for step in range(1, count)]


def mate_of(index):
    return index + 1 - 2 * lax.rem(index, 2)


def sort_tables(cols, rows, count, columns):
    slots = cols.shape[1]
    shape = (slots, slots)
    lane = lax.broadcasted_iota(jnp.int32, shape, 1)
    sublane = lax.broadcasted_iota(jnp.int32, shape, 0)
    diagonal = lane == sublane
    here = jnp.broadcast_to(cols, shape)
    key = jnp.where(lane < count, here, columns)

    def upright(value):
        return jnp.sum(jnp.where(diagonal, value, 0), axis=1, keepdims=True)

    mine = upright(key)
    row = upright(jnp.broadcast_to(rows, shape))
    earlier = (key == mine) & (lane < sublane)
    rank = jnp.sum(jnp.where((key < mine) | earlier, 1, 0), axis=1, keepdims=True)
    keep = jnp.max(jnp.where(earlier, 1, 0), axis=1, keepdims=True)
    placed = rank == lane

    def in_order(value):
        return jnp.sum(jnp.where(placed, value, 0), axis=0, keepdims=True)

    first = jnp.sum(jnp.where(mine < lane, 1, 0), axis=0, keepdims=True)
    last = jnp.sum(jnp.where(mine <= lane, 1, 0), axis=0, keepdims=True)
    return in_order(sublane), in_order(row), in_order(keep), first, last


def layer_kernel(
    outer,
    inner,
    cols,
    rows_hbm,
    cols_hbm,
    count_ref,
    grad_hbm,
    mask_hbm,
    vals_hbm,
    feat_hbm,
    weight_hbm,
    node_out_hbm,
    weight_out_hbm,
    grad_ref,
    mask_ref,
    masked_ref,
    held,
    tile_rows_ref,
    tile_cols_ref,
    table_ref,
    table,
    sums,
    part_ref,
    feat_ref,
    weight_ref,
    node_out_ref,
    pair_recv,
    pair_sum,
    line_recv,
    local_grad,
    col_recv,
    row_recv,
    whole_grad,
    load_sem,
    tile_sem,
    table_sem,
    store_sem,
    send_sem,
    pass_sem,
    recv_sem,
    pair_send_sem,
    pair_recv_sem,
    line_send_sem,
    line_recv_sem,
    col_send_sem,
    col_recv_sem,
    row_send_sem,
    row_recv_sem,
    all_send_sem,
    all_recv_sem,
    feat_send_sem,
    feat_recv_sem,
):
    row, col = lax.axis_index("row"), lax.axis_index("col")
    rows = outer * inner
    my_outer, my_inner = lax.div(row, inner), lax.rem(row, inner)
    slots, side = held.shape[0], held.shape[-1]
    width, nodes = part_ref.shape[1:]
    per_block = nodes // side
    columns = rows * per_block
    sends = []

    def start(copy):
        copy.start()
        sends.append(copy)

    def arrived(slot, sem):
        remote(slot, slot, sem, sem, (row, mate_of(col))).wait_recv()

    if outer == 4:
        across = lax.rem(my_outer + 2, outer)
        order = [across, mate_of(across), mate_of(my_outer), my_outer]
    else:
        order = others(my_outer, outer) + [my_outer]

    loads = [
        pltpu.make_async_copy(source, target, load_sem.at[index])
        for index, (source, target) in enumerate(
            [
                (grad_hbm, grad_ref),
                (mask_hbm, mask_ref),
                (rows_hbm, tile_rows_ref),
                (cols_hbm, tile_cols_ref),
                (feat_hbm, feat_ref.at[my_outer]),
                (weight_hbm, weight_ref),
            ]
        )
    ]
    for load in loads:
        load.start()
    tile_loads = []
    for index in range(slots // CHUNK):
        piece = pl.ds(index * CHUNK, CHUNK)
        load = pltpu.make_async_copy(vals_hbm.at[piece], held.at[piece], tile_sem.at[index])
        load.start()
        tile_loads.append(load)
    greet(
        [(row, peer) for peer in others(col, cols)] + [(peer, col) for peer in others(row, rows)]
    )

    loads[0].wait()
    loads[1].wait()
    mate = mate_of(col)
    far = [lax.rem(col + 2 * step, cols) for step in range(1, cols // 2)]
    row_tiles = masked_ref.shape[0]
    size = row_tiles // PARTS
    own_width = grad_ref.shape[0]

    def masked_piece(block, part):
        lines = pl.ds(pl.multiple_of(block * own_width, own_width), own_width)
        return masked_ref.at[part * size : (part + 1) * size, lines]

    def send_masked(block, part, sems, peer):
        ref = masked_piece(block, part)
        start(remote(ref, ref, sems.at[peer, part], recv_sem.at[block, part], (row, peer)))

    def masked_arrived(block, part):
        arrived(masked_piece(block, part), recv_sem.at[block, part])

    for part in range(PARTS):
        for tile in range(part * size, (part + 1) * size):
            lanes = slice(tile * side, (tile + 1) * side)
            lines = pl.ds(pl.multiple_of(col * own_width, own_width), own_width)
            masked_ref[tile, lines, :] = (
                grad_ref[:, lanes].astype(jnp.float32) * mask_ref[:, lanes].astype(jnp.float32)
            ).astype(jnp.bfloat16)
        for peer in far:
            send_masked(col, part, send_sem, peer)
    for part in range(PARTS):
        send_masked(col, part, send_sem, mate)
    for peer in order[:-1]:
        start(
            remote(
                feat_hbm,
                feat_ref.at[my_outer],
                feat_send_sem.at[peer],
                feat_recv_sem.at[my_outer],
                (peer * inner + my_inner, col),
            )
        )
    loads[2].wait()
    loads[3].wait()
    for index, line in enumerate(
        sort_tables(tile_cols_ref[...], tile_rows_ref[...], count_ref[0, 0], columns)
    ):
        table_ref[index : index + 1, :] = line
    to_scalars = pltpu.make_async_copy(table_ref, table, table_sem.at[0])
    to_scalars.start()
    for part in range(PARTS):
        for peer in far:
            masked_arrived(peer, part)
            send_masked(peer, part, pass_sem, mate)
    to_scalars.wait()
    for load in tile_loads + loads[4:]:
        load.wait()
    for part in range(PARTS):
        masked_arrived(mate, part)
        for peer in far:
            masked_arrived(mate_of(peer), part)

    def chunk_step(index, running):
        for step in range(CHUNK):
            place = index * CHUNK + step
            product = jnp.dot(
                masked_ref[table[1, place]],
                held[table[0, place]],
                preferred_element_type=jnp.float32,
            )
            running = running * table[2, place].astype(jnp.float32) + product
            sums[place] = running.astype(jnp.bfloat16)
        return running

    lax.fori_loop(0, slots // CHUNK, chunk_step, jnp.zeros((width, side), jnp.float32))

    def pack(block):
        for part in range(per_block):
            column = block * per_block + part
            begin, end = table[3, column], table[4, column]
            used = jnp.minimum(end - begin, 1).astype(jnp.float32)
            value = sums[jnp.maximum(end - 1, 0)].astype(jnp.float32) * used
            part_ref[block, :, part * side : (part + 1) * side] = value.astype(jnp.bfloat16)

    height = width // HALVES
    steps = [(block, half) for block in order for half in range(HALVES)]

    def strip(half):
        return pl.ds(half * height, height)

    def pair_sends(step):
        block, half = steps[step]
        return [
            remote(
                part_ref.at[block * inner + peer, strip(half)],
                pair_recv.at[my_inner, block, strip(half)],
                pair_send_sem.at[peer, block, half],
                pair_recv_sem.at[my_inner, block, half],
                (my_outer * inner + peer, col),
            )
            for peer in others(my_inner, inner)
        ]

    for index, block in enumerate(order):
        for peer in others(my_inner, inner):
            pack(block * inner + peer)
        if index == 0:
            for step in range(2):
                for copy in pair_sends(step):
                    copy.start()
    for block in order:
        pack(block * inner + my_inner)
    values = []
    grads = [0.0] * HALVES
    for step, (block, half) in enumerate(steps):
        for copy in pair_sends(step):
            copy.wait_send()
        if step + 2 < len(steps):
            for copy in pair_sends(step + 2):
                copy.start()
        value = part_ref[block * inner + my_inner, strip(half)].astype(jnp.float32)
        for peer in others(my_inner, inner):
            arrived(pair_recv.at[peer, block, strip(half)], pair_recv_sem.at[peer, block, half])
            value += pair_recv[peer, block, strip(half)].astype(jnp.float32)
        rounded = value.astype(jnp.bfloat16)
        if block is my_outer:
            values.append(value)
        else:
            pair_sum[block, strip(half)] = rounded
            start(
                remote(
                    pair_sum.at[block, strip(half)],
                    line_recv.at[my_outer, strip(half)],
                    line_send_sem.at[block, half],
                    line_recv_sem.at[my_outer, half],
                    (block * inner + my_inner, col),
                )
            )
            if half == 0:
                arrived(feat_ref.at[block], feat_recv_sem.at[block])
        grads[half] += jnp.dot(rounded, feat_ref[block], preferred_element_type=jnp.float32)
    local_grad[...] = jnp.concatenate(grads, axis=0).T
    piece = local_grad.shape[0] // cols

    def rows_of(ref, index):
        return ref.at[pl.ds(pl.multiple_of(index * piece, piece), piece)]

    for peer in others(col, cols):
        start(
            remote(
                rows_of(local_grad, peer),
                col_recv.at[col],
                col_send_sem.at[peer],
                col_recv_sem.at[col],
                (row, peer),
            )
        )
    piece_sum = rows_of(local_grad, col)[...]
    for peer in others(col, cols):
        arrived(col_recv.at[peer], col_recv_sem.at[peer])
        piece_sum += col_recv[peer]
    row_recv[row] = piece_sum.astype(jnp.bfloat16)
    for peer in others(row, rows):
        start(
            remote(
                row_recv.at[row],
                row_recv.at[row],
                row_send_sem.at[peer],
                row_recv_sem.at[row],
                (peer, col),
            )
        )
    for half in range(HALVES):
        for peer in reversed(order[:-1]):
            arrived(line_recv.at[peer, strip(half)], line_recv_sem.at[peer, half])
            values[half] += line_recv[peer, strip(half)].astype(jnp.float32)
    aggregate = jnp.concatenate(values, axis=0).astype(jnp.bfloat16)
    node_out_ref[...] = (
        jnp.dot(weight_ref[...], aggregate, preferred_element_type=jnp.float32)
        .T.astype(jnp.bfloat16)
    )
    node_store = pltpu.make_async_copy(node_out_ref, node_out_hbm, store_sem.at[0])
    node_store.start()
    for peer in others(row, rows):
        arrived(row_recv.at[peer], row_recv_sem.at[peer])
    piece_sum = row_recv[0].astype(jnp.float32)
    for index in range(1, rows):
        piece_sum += row_recv[index].astype(jnp.float32)
    rows_of(whole_grad, col)[...] = piece_sum
    for peer in others(col, cols):
        start(
            remote(
                rows_of(whole_grad, col),
                rows_of(whole_grad, col),
                all_send_sem.at[peer],
                all_recv_sem.at[col],
                (row, peer),
            )
        )
    for peer in others(col, cols):
        arrived(rows_of(whole_grad, peer), all_recv_sem.at[peer])
    weight_store = pltpu.make_async_copy(whole_grad, weight_out_hbm, store_sem.at[1])
    weight_store.start()
    for copy in sends:
        copy.wait_send()
    node_store.wait()
    weight_store.wait()


def finish_kernel(
    node_hbm, grad_hbm, imp_hbm, delta_hbm, node_out, imp_out, node_ref, grad_ref, imp_ref, delta_ref, sems
):
    loads = [
        pltpu.make_async_copy(source, target, sems.at[index])
        for index, (source, target) in enumerate(
            [(node_hbm, node_ref), (grad_hbm, grad_ref), (imp_hbm, imp_ref), (delta_hbm, delta_ref)]
        )
    ]
    for load in loads:
        load.start()
    loads[0].wait()
    node_store = pltpu.make_async_copy(node_ref, node_out, sems.at[4])
    node_store.start()
    for load in loads[1:]:
        load.wait()
    imp_ref[...] = imp_ref[...] - grad_ref[...] * delta_ref[...]
    imp_store = pltpu.make_async_copy(imp_ref, imp_out, sems.at[5])
    imp_store.start()
    node_store.wait()
    imp_store.wait()


def local(
    rows,
    cols,
    tile_vals,
    tile_row,
    tile_col,
    tile_count,
    out_grad,
    relu_mask,
    features,
    weight,
    importance,
    weight_delta,
):
    slots, side = tile_vals.shape[2], tile_vals.shape[-1]
    nodes, depth = features.shape
    block_nodes, own_width = out_grad.shape
    width = own_width * cols
    inner = 2 if rows % 2 == 0 else 1
    outer = rows // inner
    params = functools.partial(pltpu.CompilerParams, vmem_limit_bytes=60 * 2**20)
    dma = pltpu.SemaphoreType.DMA
    piece = depth // cols
    bf16 = jnp.bfloat16
    f32 = jnp.float32
    i32 = jnp.int32

    node_grad, weight_grad = pl.pallas_call(
        functools.partial(layer_kernel, outer, inner, cols),
        out_shape=(
            jax.ShapeDtypeStruct((nodes, depth), bf16),
            jax.ShapeDtypeStruct((depth, width), f32),
        ),
        in_specs=[HBM, HBM, SMEM] + [HBM] * 5,
        out_specs=(HBM, HBM),
        scratch_shapes=[
            pltpu.VMEM((own_width, block_nodes), bf16),
            pltpu.VMEM((own_width, block_nodes), i32),
            pltpu.VMEM((block_nodes // side, width, side), bf16),
            pltpu.VMEM((slots, side, side), bf16),
            pltpu.VMEM((1, slots), i32),
            pltpu.VMEM((1, slots), i32),
            pltpu.VMEM((8, slots), i32),
            pltpu.SMEM((8, slots), i32),
            pltpu.VMEM((slots, width, side), bf16),
            pltpu.VMEM((rows, width, nodes), bf16),
            pltpu.VMEM((outer, nodes, depth), bf16),
            pltpu.VMEM((depth, width), bf16),
            pltpu.VMEM((nodes, depth), bf16),
            pltpu.VMEM((inner, outer, width, nodes), bf16),
            pltpu.VMEM((outer, width, nodes), bf16),
            pltpu.VMEM((outer, width, nodes), bf16),
            pltpu.VMEM((depth, width), f32),
            pltpu.VMEM((cols, piece, width), f32),
            pltpu.VMEM((rows, piece, width), bf16),
            pltpu.VMEM((depth, width), f32),
            dma((6,)),
            dma((slots // CHUNK,)),
            dma((1,)),
            dma((2,)),
            dma((cols, PARTS)),
            dma((cols, PARTS)),
            dma((cols, PARTS)),
            dma((inner, outer, HALVES)),
            dma((inner, outer, HALVES)),
            dma((outer, HALVES)),
            dma((outer, HALVES)),
            dma((cols,)),
            dma((cols,)),
            dma((rows,)),
            dma((rows,)),
            dma((cols,)),
            dma((cols,)),
            dma((outer,)),
            dma((outer,)),
        ],
        compiler_params=params(collective_id=0, has_side_effects=True),
        name="layer_backward",
    )(
        tile_row.reshape(1, slots),
        tile_col.reshape(1, slots),
        tile_count,
        out_grad.T,
        relu_mask.T,
        tile_vals.reshape(slots, side, side),
        features,
        weight,
    )

    return pl.pallas_call(
        finish_kernel,
        out_shape=(
            jax.ShapeDtypeStruct((nodes, depth), bf16),
            jax.ShapeDtypeStruct((depth, width), f32),
        ),
        in_specs=[HBM] * 4,
        out_specs=(HBM, HBM),
        scratch_shapes=[
            pltpu.VMEM((nodes, depth), bf16),
            pltpu.VMEM((depth, width), f32),
            pltpu.VMEM((depth, width), f32),
            pltpu.VMEM((depth, width), f32),
            dma((6,)),
        ],
        compiler_params=params(),
        name="finish",
    )(node_grad, weight_grad, importance, weight_delta)


def solution(mesh):
    return jax.shard_map(
        functools.partial(local, mesh.shape["row"], mesh.shape["col"]),
        mesh=mesh,
        in_specs=(
            P("row", "col", None, None, None),
            P("row", "col", None),
            P("row", "col", None),
            P("row", "col"),
            P("row", "col"),
            P("row", "col"),
            P(("row", "col"), None),
            P(),
            P(),
            P(),
        ),
        out_specs=(P(("row", "col"), None), P()),
        check_vma=False,
    )
```

```python
import functools

import jax
import jax.numpy as jnp
from jax import lax
from jax.experimental import pallas as pl
from jax.experimental.pallas import tpu as pltpu
from jax.sharding import PartitionSpec as P

MESH = pl.DeviceIdType.MESH
SMEM = pl.BlockSpec(memory_space=pltpu.SMEM)
HBM = pl.BlockSpec(memory_space=pltpu.HBM)
PARTS = 4
CHUNK = 16


def remote(src, dst, send_sem, recv_sem, device):
    return pltpu.make_async_remote_copy(
        src_ref=src,
        dst_ref=dst,
        send_sem=send_sem,
        recv_sem=recv_sem,
        device_id=device,
        device_id_type=MESH,
    )


def others(me, count):
    return [lax.rem(me + step, count) for step in range(1, count)]


def mate_of(index):
    return index + 1 - 2 * lax.rem(index, 2)


def sort_tables(cols, rows, count, columns):
    slots = cols.shape[1]
    shape = (slots, slots)
    lane = lax.broadcasted_iota(jnp.int32, shape, 1)
    sublane = lax.broadcasted_iota(jnp.int32, shape, 0)
    diagonal = lane == sublane
    here = jnp.broadcast_to(cols, shape)
    key = jnp.where(lane < count, here, columns)

    def upright(value):
        return jnp.sum(jnp.where(diagonal, value, 0), axis=1, keepdims=True)

    mine = upright(key)
    row = upright(jnp.broadcast_to(rows, shape))
    earlier = (key == mine) & (lane < sublane)
    rank = jnp.sum(jnp.where((key < mine) | earlier, 1, 0), axis=1, keepdims=True)
    keep = jnp.max(jnp.where(earlier, 1, 0), axis=1, keepdims=True)
    placed = rank == lane

    def in_order(value):
        return jnp.sum(jnp.where(placed, value, 0), axis=0, keepdims=True)

    first = jnp.sum(jnp.where(mine < lane, 1, 0), axis=0, keepdims=True)
    last = jnp.sum(jnp.where(mine <= lane, 1, 0), axis=0, keepdims=True)
    return in_order(sublane), in_order(row), in_order(keep), first, last


def layer_kernel(
    outer,
    inner,
    cols,
    rows_hbm,
    cols_hbm,
    count_ref,
    grad_hbm,
    mask_hbm,
    vals_hbm,
    feat_hbm,
    weight_hbm,
    node_out_hbm,
    weight_out_hbm,
    grad_ref,
    mask_ref,
    near_ref,
    far_ref,
    held,
    tile_rows_ref,
    tile_cols_ref,
    table_ref,
    table,
    near_sums,
    far_sums,
    part_ref,
    feat_ref,
    weight_ref,
    node_out_ref,
    pair_recv,
    pair_sum,
    line_recv,
    local_grad,
    col_recv,
    row_recv,
    whole_grad,
    aggregate,
    load_sem,
    tile_sem,
    table_sem,
    store_sem,
    send_sem,
    pass_sem,
    recv_sem,
    pair_send_sem,
    pair_recv_sem,
    line_send_sem,
    line_recv_sem,
    col_send_sem,
    col_recv_sem,
    row_send_sem,
    row_recv_sem,
    all_send_sem,
    all_recv_sem,
    feat_send_sem,
    feat_recv_sem,
):
    row, col = lax.axis_index("row"), lax.axis_index("col")
    rows = outer * inner
    my_outer, my_inner = lax.div(row, inner), lax.rem(row, inner)
    slots, side = held.shape[0], held.shape[-1]
    width, nodes = part_ref.shape[1:]
    per_block = nodes // side
    columns = rows * per_block
    sends = []

    def start(copy):
        copy.start()
        sends.append(copy)

    def arrived(slot, sem):
        remote(slot, slot, sem, sem, (row, mate_of(col))).wait_recv()

    if outer == 4:
        across = lax.rem(my_outer + 2, outer)
        order = [across, mate_of(across), mate_of(my_outer), my_outer]
    else:
        order = others(my_outer, outer) + [my_outer]

    loads = [
        pltpu.make_async_copy(source, target, load_sem.at[index])
        for index, (source, target) in enumerate(
            [
                (grad_hbm, grad_ref),
                (mask_hbm, mask_ref),
                (rows_hbm, tile_rows_ref),
                (cols_hbm, tile_cols_ref),
                (feat_hbm, feat_ref.at[my_outer]),
                (weight_hbm, weight_ref),
            ]
        )
    ]
    for load in loads:
        load.start()
    tile_loads = []
    for index in range(slots // CHUNK):
        piece = pl.ds(index * CHUNK, CHUNK)
        load = pltpu.make_async_copy(vals_hbm.at[piece], held.at[piece], tile_sem.at[index])
        load.start()
        tile_loads.append(load)
    partners = [(row, peer) for peer in others(col, cols)] + [
        (peer, col) for peer in others(row, rows)
    ]
    barrier = pltpu.get_barrier_semaphore()
    for partner in partners:
        pl.semaphore_signal(barrier, inc=1, device_id=partner, device_id_type=MESH)

    loads[2].wait()
    loads[3].wait()
    for index, line in enumerate(
        sort_tables(tile_cols_ref[...], tile_rows_ref[...], count_ref[0, 0], columns)
    ):
        table_ref[index : index + 1, :] = line
    to_scalars = pltpu.make_async_copy(table_ref, table, table_sem.at[0])
    to_scalars.start()

    loads[0].wait()
    loads[1].wait()
    mate = mate_of(col)
    first = col - lax.rem(col, 2)
    far = [lax.rem(col + 2 * step, cols) for step in range(1, cols // 2)]
    row_tiles = near_ref.shape[0]
    size = row_tiles // PARTS
    own_width = grad_ref.shape[0]

    def tiles_of(part):
        return pl.ds(part * size, size)

    def lines_of(position):
        return pl.ds(pl.multiple_of(position * own_width, own_width), own_width)

    def near_piece(block, part):
        return near_ref.at[tiles_of(part), lines_of(lax.rem(block, 2))]

    def far_piece(block, part, device):
        position = lax.rem(block - (device - lax.rem(device, 2)) + cols, cols) - 2
        return far_ref.at[tiles_of(part), lines_of(position)]

    for tile in range(row_tiles):
        lanes = slice(tile * side, (tile + 1) * side)
        near_ref[tile, lines_of(lax.rem(col, 2)), :] = (
            grad_ref[:, lanes].astype(jnp.float32) * mask_ref[:, lanes].astype(jnp.float32)
        ).astype(jnp.bfloat16)
    pl.semaphore_wait(barrier, len(partners))
    for part in range(PARTS):
        for peer in far:
            start(
                remote(
                    near_piece(col, part),
                    far_piece(col, part, peer),
                    send_sem.at[peer, part],
                    recv_sem.at[col, part],
                    (row, peer),
                )
            )
        ref = near_piece(col, part)
        start(remote(ref, ref, send_sem.at[mate, part], recv_sem.at[col, part], (row, mate)))
    for peer in order[:-1]:
        start(
            remote(
                feat_hbm,
                feat_ref.at[my_outer],
                feat_send_sem.at[peer],
                feat_recv_sem.at[my_outer],
                (peer * inner + my_inner, col),
            )
        )

    def products(masked_ref, sums, begin, end, running):
        def chunk_step(index, running):
            for step in range(CHUNK):
                place = index * CHUNK + step
                product = jnp.dot(
                    masked_ref[table[1, place]],
                    held[table[0, place]],
                    preferred_element_type=jnp.float32,
                )
                running = running * table[2, place].astype(jnp.float32) + product
                sums[place] = running.astype(jnp.bfloat16)
            return running

        return lax.fori_loop(begin, end, chunk_step, running)

    near = near_ref.shape[1]
    strips = [pl.ds(0, near), pl.ds(near, width - near)]

    def pack(sums, strip, block):
        for part in range(per_block):
            column = block * per_block + part
            begin, end = table[3, column], table[4, column]
            used = jnp.minimum(end - begin, 1).astype(jnp.float32)
            value = sums[jnp.maximum(end - 1, 0)].astype(jnp.float32) * used
            part_ref[block, strip, part * side : (part + 1) * side] = value.astype(jnp.bfloat16)

    to_scalars.wait()
    for load in tile_loads + loads[4:]:
        load.wait()
    for part in range(PARTS):
        arrived(near_piece(mate, part), recv_sem.at[mate, part])
    chunks = slots // CHUNK
    pause = chunks * 3 // 4
    zeros = jnp.zeros((near, side), jnp.float32)
    running = products(near_ref, near_sums, 0, pause, zeros)
    for part in range(PARTS):
        for peer in far:
            ref = far_piece(peer, part, col)
            arrived(ref, recv_sem.at[peer, part])
            start(remote(ref, ref, pass_sem.at[peer, part], recv_sem.at[peer, part], (row, mate)))
    products(near_ref, near_sums, pause, chunks, running)

    steps = [(block, half) for half in range(2) for block in order]

    def strip(half):
        return strips[half]

    def pair_sends(step):
        block, half = steps[step]
        return [
            remote(
                part_ref.at[block * inner + peer, strip(half)],
                pair_recv.at[my_inner, block, strip(half)],
                pair_send_sem.at[peer, block, half],
                pair_recv_sem.at[my_inner, block, half],
                (my_outer * inner + peer, col),
            )
            for peer in others(my_inner, inner)
        ]

    for step, block in enumerate(order):
        for peer in others(my_inner, inner):
            pack(near_sums, strips[0], block * inner + peer)
        for copy in pair_sends(step):
            copy.start()
    for part in range(PARTS):
        for peer in far:
            block = mate_of(peer)
            arrived(far_piece(block, part, col), recv_sem.at[block, part])
    products(far_ref, far_sums, 0, chunks, jnp.zeros((width - near, side), jnp.float32))
    for index, block in enumerate(order):
        for peer in others(my_inner, inner):
            pack(far_sums, strips[1], block * inner + peer)
        if index < 2:
            for copy in pair_sends(outer + index):
                copy.start()
    for block in order:
        pack(near_sums, strips[0], block * inner + my_inner)
        pack(far_sums, strips[1], block * inner + my_inner)
    values = []
    grads = [0.0] * 2
    for step, (block, half) in enumerate(steps):
        for copy in pair_sends(step):
            copy.wait_send()
        if outer <= step < len(steps) - 2:
            for copy in pair_sends(step + 2):
                copy.start()
        value = part_ref[block * inner + my_inner, strip(half)].astype(jnp.float32)
        for peer in others(my_inner, inner):
            arrived(pair_recv.at[peer, block, strip(half)], pair_recv_sem.at[peer, block, half])
            value += pair_recv[peer, block, strip(half)].astype(jnp.float32)
        rounded = value.astype(jnp.bfloat16)
        if block is my_outer:
            values.append(value)
        else:
            pair_sum[block, strip(half)] = rounded
            start(
                remote(
                    pair_sum.at[block, strip(half)],
                    line_recv.at[my_outer, strip(half)],
                    line_send_sem.at[block, half],
                    line_recv_sem.at[my_outer, half],
                    (block * inner + my_inner, col),
                )
            )
            if half == 0:
                arrived(feat_ref.at[block], feat_recv_sem.at[block])
        grads[half] += jnp.dot(rounded, feat_ref[block], preferred_element_type=jnp.float32)
    turned = jnp.concatenate(grads, axis=0)
    for position in range(cols):
        whole_grad[lines_of(lax.rem(position + first, cols)), :] = turned[
            position * own_width : (position + 1) * own_width
        ]
    local_grad[...] = whole_grad[...].T
    piece = local_grad.shape[0] // cols

    def rows_of(ref, index):
        return ref.at[pl.ds(pl.multiple_of(index * piece, piece), piece)]

    for peer in others(col, cols):
        start(
            remote(
                rows_of(local_grad, peer),
                col_recv.at[col],
                col_send_sem.at[peer],
                col_recv_sem.at[col],
                (row, peer),
            )
        )
    piece_sum = rows_of(local_grad, col)[...]
    for peer in others(col, cols):
        arrived(col_recv.at[peer], col_recv_sem.at[peer])
        piece_sum += col_recv[peer]
    row_recv[row] = piece_sum.astype(jnp.bfloat16)
    for peer in others(row, rows):
        start(
            remote(
                row_recv.at[row],
                row_recv.at[row],
                row_send_sem.at[peer],
                row_recv_sem.at[row],
                (peer, col),
            )
        )
    for half in range(2):
        for peer in reversed(order[:-1]):
            arrived(line_recv.at[peer, strip(half)], line_recv_sem.at[peer, half])
            values[half] += line_recv[peer, strip(half)].astype(jnp.float32)
    turned = jnp.concatenate(values, axis=0).astype(jnp.bfloat16)
    for position in range(cols):
        aggregate[lines_of(lax.rem(position + first, cols)), :] = turned[
            position * own_width : (position + 1) * own_width
        ]
    node_out_ref[...] = (
        jnp.dot(weight_ref[...], aggregate[...], preferred_element_type=jnp.float32)
        .T.astype(jnp.bfloat16)
    )
    node_store = pltpu.make_async_copy(node_out_ref, node_out_hbm, store_sem.at[0])
    node_store.start()
    for peer in others(row, rows):
        arrived(row_recv.at[peer], row_recv_sem.at[peer])
    piece_sum = row_recv[0].astype(jnp.float32)
    for index in range(1, rows):
        piece_sum += row_recv[index].astype(jnp.float32)
    rows_of(whole_grad, col)[...] = piece_sum
    for peer in others(col, cols):
        start(
            remote(
                rows_of(whole_grad, col),
                rows_of(whole_grad, col),
                all_send_sem.at[peer],
                all_recv_sem.at[col],
                (row, peer),
            )
        )
    for peer in others(col, cols):
        arrived(rows_of(whole_grad, peer), all_recv_sem.at[peer])
    weight_store = pltpu.make_async_copy(whole_grad, weight_out_hbm, store_sem.at[1])
    weight_store.start()
    for copy in sends:
        copy.wait_send()
    node_store.wait()
    weight_store.wait()


def finish_kernel(
    node_hbm, grad_hbm, imp_hbm, delta_hbm, node_out, imp_out, node_ref, grad_ref, imp_ref, delta_ref, sems
):
    loads = [
        pltpu.make_async_copy(source, target, sems.at[index])
        for index, (source, target) in enumerate(
            [(node_hbm, node_ref), (grad_hbm, grad_ref), (imp_hbm, imp_ref), (delta_hbm, delta_ref)]
        )
    ]
    for load in loads:
        load.start()
    loads[0].wait()
    node_store = pltpu.make_async_copy(node_ref, node_out, sems.at[4])
    node_store.start()
    for load in loads[1:]:
        load.wait()
    imp_ref[...] = imp_ref[...] - grad_ref[...] * delta_ref[...]
    imp_store = pltpu.make_async_copy(imp_ref, imp_out, sems.at[5])
    imp_store.start()
    node_store.wait()
    imp_store.wait()


def local(
    rows,
    cols,
    tile_vals,
    tile_row,
    tile_col,
    tile_count,
    out_grad,
    relu_mask,
    features,
    weight,
    importance,
    weight_delta,
):
    slots, side = tile_vals.shape[2], tile_vals.shape[-1]
    nodes, depth = features.shape
    block_nodes, own_width = out_grad.shape
    width = own_width * cols
    inner = 2 if rows % 2 == 0 else 1
    outer = rows // inner
    params = functools.partial(pltpu.CompilerParams, vmem_limit_bytes=60 * 2**20)
    dma = pltpu.SemaphoreType.DMA
    piece = depth // cols
    bf16 = jnp.bfloat16
    f32 = jnp.float32
    i32 = jnp.int32

    node_grad, weight_grad = pl.pallas_call(
        functools.partial(layer_kernel, outer, inner, cols),
        out_shape=(
            jax.ShapeDtypeStruct((nodes, depth), bf16),
            jax.ShapeDtypeStruct((depth, width), f32),
        ),
        in_specs=[HBM, HBM, SMEM] + [HBM] * 5,
        out_specs=(HBM, HBM),
        scratch_shapes=[
            pltpu.VMEM((own_width, block_nodes), bf16),
            pltpu.VMEM((own_width, block_nodes), i32),
            pltpu.VMEM((block_nodes // side, 2 * own_width, side), bf16),
            pltpu.VMEM((block_nodes // side, width - 2 * own_width, side), bf16),
            pltpu.VMEM((slots, side, side), bf16),
            pltpu.VMEM((1, slots), i32),
            pltpu.VMEM((1, slots), i32),
            pltpu.VMEM((8, slots), i32),
            pltpu.SMEM((8, slots), i32),
            pltpu.VMEM((slots, 2 * own_width, side), bf16),
            pltpu.VMEM((slots, width - 2 * own_width, side), bf16),
            pltpu.VMEM((rows, width, nodes), bf16),
            pltpu.VMEM((outer, nodes, depth), bf16),
            pltpu.VMEM((depth, width), bf16),
            pltpu.VMEM((nodes, depth), bf16),
            pltpu.VMEM((inner, outer, width, nodes), bf16),
            pltpu.VMEM((outer, width, nodes), bf16),
            pltpu.VMEM((outer, width, nodes), bf16),
            pltpu.VMEM((depth, width), f32),
            pltpu.VMEM((cols, piece, width), f32),
            pltpu.VMEM((rows, piece, width), bf16),
            pltpu.VMEM((depth, width), f32),
            pltpu.VMEM((width, nodes), bf16),
            dma((6,)),
            dma((slots // CHUNK,)),
            dma((1,)),
            dma((2,)),
            dma((cols, PARTS)),
            dma((cols, PARTS)),
            dma((cols, PARTS)),
            dma((inner, outer, 2)),
            dma((inner, outer, 2)),
            dma((outer, 2)),
            dma((outer, 2)),
            dma((cols,)),
            dma((cols,)),
            dma((rows,)),
            dma((rows,)),
            dma((cols,)),
            dma((cols,)),
            dma((outer,)),
            dma((outer,)),
        ],
        compiler_params=params(collective_id=0, has_side_effects=True),
        name="layer_backward",
    )(
        tile_row.reshape(1, slots),
        tile_col.reshape(1, slots),
        tile_count,
        out_grad.T,
        relu_mask.T,
        tile_vals.reshape(slots, side, side),
        features,
        weight,
    )

    return pl.pallas_call(
        finish_kernel,
        out_shape=(
            jax.ShapeDtypeStruct((nodes, depth), bf16),
            jax.ShapeDtypeStruct((depth, width), f32),
        ),
        in_specs=[HBM] * 4,
        out_specs=(HBM, HBM),
        scratch_shapes=[
            pltpu.VMEM((nodes, depth), bf16),
            pltpu.VMEM((depth, width), f32),
            pltpu.VMEM((depth, width), f32),
            pltpu.VMEM((depth, width), f32),
            dma((6,)),
        ],
        compiler_params=params(),
        name="finish",
    )(node_grad, weight_grad, importance, weight_delta)


def solution(mesh):
    return jax.shard_map(
        functools.partial(local, mesh.shape["row"], mesh.shape["col"]),
        mesh=mesh,
        in_specs=(
            P("row", "col", None, None, None),
            P("row", "col", None),
            P("row", "col", None),
            P("row", "col"),
            P("row", "col"),
            P("row", "col"),
            P(("row", "col"), None),
            P(),
            P(),
            P(),
        ),
        out_specs=(P(("row", "col"), None), P()),
        check_vma=False,
    )
```

```python
import functools

import jax
import jax.numpy as jnp
from jax import lax
from jax.experimental import pallas as pl
from jax.experimental.pallas import tpu as pltpu
from jax.sharding import PartitionSpec as P

MESH = pl.DeviceIdType.MESH
SMEM = pl.BlockSpec(memory_space=pltpu.SMEM)
HBM = pl.BlockSpec(memory_space=pltpu.HBM)
PARTS = 4
CHUNK = 16


def remote(src, dst, send_sem, recv_sem, device):
    return pltpu.make_async_remote_copy(
        src_ref=src,
        dst_ref=dst,
        send_sem=send_sem,
        recv_sem=recv_sem,
        device_id=device,
        device_id_type=MESH,
    )


def others(me, count):
    return [lax.rem(me + step, count) for step in range(1, count)]


def mate_of(index):
    return index + 1 - 2 * lax.rem(index, 2)


def sort_tables(cols, rows, count, columns):
    slots = cols.shape[1]
    shape = (slots, slots)
    lane = lax.broadcasted_iota(jnp.int32, shape, 1)
    sublane = lax.broadcasted_iota(jnp.int32, shape, 0)
    diagonal = lane == sublane
    here = jnp.broadcast_to(cols, shape)
    key = jnp.where(lane < count, here, columns)

    def upright(value):
        return jnp.sum(jnp.where(diagonal, value, 0), axis=1, keepdims=True)

    mine = upright(key)
    row = upright(jnp.broadcast_to(rows, shape))
    earlier = (key == mine) & (lane < sublane)
    rank = jnp.sum(jnp.where((key < mine) | earlier, 1, 0), axis=1, keepdims=True)
    keep = jnp.max(jnp.where(earlier, 1, 0), axis=1, keepdims=True)
    placed = rank == lane

    def in_order(value):
        return jnp.sum(jnp.where(placed, value, 0), axis=0, keepdims=True)

    first = jnp.sum(jnp.where(mine < lane, 1, 0), axis=0, keepdims=True)
    last = jnp.sum(jnp.where(mine <= lane, 1, 0), axis=0, keepdims=True)
    return in_order(sublane), in_order(row), in_order(keep), first, last


def layer_kernel(
    outer,
    inner,
    cols,
    rows_hbm,
    cols_hbm,
    count_ref,
    grad_hbm,
    mask_hbm,
    vals_hbm,
    feat_hbm,
    weight_hbm,
    node_out_hbm,
    weight_out_hbm,
    grad_ref,
    mask_ref,
    near_ref,
    far_ref,
    held,
    tile_rows_ref,
    tile_cols_ref,
    table_ref,
    table,
    near_sums,
    far_sums,
    part_ref,
    feat_ref,
    weight_ref,
    node_out_ref,
    pair_recv,
    pair_sum,
    line_recv,
    local_grad,
    col_recv,
    row_recv,
    whole_grad,
    aggregate,
    load_sem,
    tile_sem,
    table_sem,
    store_sem,
    send_sem,
    pass_sem,
    recv_sem,
    pair_send_sem,
    pair_recv_sem,
    line_send_sem,
    line_recv_sem,
    col_send_sem,
    col_recv_sem,
    row_send_sem,
    row_recv_sem,
    all_send_sem,
    all_recv_sem,
    feat_send_sem,
    feat_recv_sem,
    hand_sem,
):
    row, col = lax.axis_index("row"), lax.axis_index("col")
    rows = outer * inner
    my_outer, my_inner = lax.div(row, inner), lax.rem(row, inner)
    slots, side = held.shape[0], held.shape[-1]
    width, nodes = part_ref.shape[1:]
    per_block = nodes // side
    columns = rows * per_block
    sends = []

    def start(copy):
        copy.start()
        sends.append(copy)

    def arrived(slot, sem):
        remote(slot, slot, sem, sem, (row, mate_of(col))).wait_recv()

    if outer == 4:
        across = lax.rem(my_outer + 2, outer)
        outer_mate = mate_of(my_outer)
        order = [across, mate_of(across), outer_mate, my_outer]
    else:
        outer_mate = None
        order = others(my_outer, outer) + [my_outer]

    loads = [
        pltpu.make_async_copy(source, target, load_sem.at[index])
        for index, (source, target) in enumerate(
            [
                (grad_hbm, grad_ref),
                (mask_hbm, mask_ref),
                (rows_hbm, tile_rows_ref),
                (cols_hbm, tile_cols_ref),
                (feat_hbm, feat_ref.at[my_outer]),
                (weight_hbm, weight_ref),
            ]
        )
    ]
    for load in loads:
        load.start()
    tile_loads = []
    for index in range(slots // CHUNK):
        piece = pl.ds(index * CHUNK, CHUNK)
        load = pltpu.make_async_copy(vals_hbm.at[piece], held.at[piece], tile_sem.at[index])
        load.start()
        tile_loads.append(load)
    partners = [(row, peer) for peer in others(col, cols)] + [
        (peer, col) for peer in others(row, rows)
    ]
    barrier = pltpu.get_barrier_semaphore()
    for partner in partners:
        pl.semaphore_signal(barrier, inc=1, device_id=partner, device_id_type=MESH)

    loads[2].wait()
    loads[3].wait()
    for index, line in enumerate(
        sort_tables(tile_cols_ref[...], tile_rows_ref[...], count_ref[0, 0], columns)
    ):
        table_ref[index : index + 1, :] = line
    to_scalars = pltpu.make_async_copy(table_ref, table, table_sem.at[0])
    to_scalars.start()

    loads[0].wait()
    loads[1].wait()
    mate = mate_of(col)
    first = col - lax.rem(col, 2)
    far = [lax.rem(col + 2 * step, cols) for step in range(1, cols // 2)]
    row_tiles = near_ref.shape[0]
    size = row_tiles // PARTS
    own_width = grad_ref.shape[0]

    def tiles_of(part):
        return pl.ds(part * size, size)

    def lines_of(position):
        return pl.ds(pl.multiple_of(position * own_width, own_width), own_width)

    def near_piece(block, part):
        return near_ref.at[tiles_of(part), lines_of(lax.rem(block, 2))]

    def far_piece(block, part, device):
        position = lax.rem(block - (device - lax.rem(device, 2)) + cols, cols) - 2
        return far_ref.at[tiles_of(part), lines_of(position)]

    for tile in range(row_tiles):
        lanes = slice(tile * side, (tile + 1) * side)
        near_ref[tile, lines_of(lax.rem(col, 2)), :] = (
            grad_ref[:, lanes].astype(jnp.float32) * mask_ref[:, lanes].astype(jnp.float32)
        ).astype(jnp.bfloat16)
    pl.semaphore_wait(barrier, len(partners))
    for part in range(PARTS):
        for peer in far:
            start(
                remote(
                    near_piece(col, part),
                    far_piece(col, part, peer),
                    send_sem.at[peer, part],
                    recv_sem.at[col, part],
                    (row, peer),
                )
            )
        ref = near_piece(col, part)
        start(remote(ref, ref, send_sem.at[mate, part], recv_sem.at[col, part], (row, mate)))
    line = outer == 4
    near_end = lax.div(lax.rem(my_outer + 1, 4), 2)
    nearer = 2 - lax.div(my_outer, 2)
    for peer in [nearer, mate_of(my_outer)] if line else order[:-1]:
        start(
            remote(
                feat_hbm,
                feat_ref.at[my_outer],
                feat_send_sem.at[peer],
                feat_recv_sem.at[my_outer],
                (peer * inner + my_inner, col),
            )
        )

    def products(masked_ref, sums, begin, end, running):
        def chunk_step(index, running):
            for step in range(CHUNK):
                place = index * CHUNK + step
                product = jnp.dot(
                    masked_ref[table[1, place]],
                    held[table[0, place]],
                    preferred_element_type=jnp.float32,
                )
                running = running * table[2, place].astype(jnp.float32) + product
                sums[place] = running.astype(jnp.bfloat16)
            return running

        return lax.fori_loop(begin, end, chunk_step, running)

    near = near_ref.shape[1]
    strips = [pl.ds(0, near), pl.ds(near, width - near)]

    def pack(sums, strip, block):
        for part in range(per_block):
            column = block * per_block + part
            begin, end = table[3, column], table[4, column]
            used = jnp.minimum(end - begin, 1).astype(jnp.float32)
            value = sums[jnp.maximum(end - 1, 0)].astype(jnp.float32) * used
            part_ref[block, strip, part * side : (part + 1) * side] = value.astype(jnp.bfloat16)

    to_scalars.wait()
    for load in tile_loads + loads[4:]:
        load.wait()
    for part in range(PARTS):
        arrived(near_piece(mate, part), recv_sem.at[mate, part])
    chunks = slots // CHUNK
    pause = chunks * 3 // 4
    zeros = jnp.zeros((near, side), jnp.float32)
    running = products(near_ref, near_sums, 0, pause, zeros)
    for part in range(PARTS):
        for peer in far:
            ref = far_piece(peer, part, col)
            arrived(ref, recv_sem.at[peer, part])
            start(remote(ref, ref, pass_sem.at[peer, part], recv_sem.at[peer, part], (row, mate)))
    products(near_ref, near_sums, pause, chunks, running)

    steps = [(block, half) for half in range(2) for block in order]

    def strip(half):
        return strips[half]

    def pair_sends(step):
        block, half = steps[step]
        return [
            remote(
                part_ref.at[block * inner + peer, strip(half)],
                pair_recv.at[my_inner, block, strip(half)],
                pair_send_sem.at[peer, block, half],
                pair_recv_sem.at[my_inner, block, half],
                (my_outer * inner + peer, col),
            )
            for peer in others(my_inner, inner)
        ]

    for step, block in enumerate(order):
        for peer in others(my_inner, inner):
            pack(near_sums, strips[0], block * inner + peer)
        for copy in pair_sends(step):
            copy.start()
    for part in range(PARTS):
        for peer in far:
            block = mate_of(peer)
            arrived(far_piece(block, part, col), recv_sem.at[block, part])
    zeros = jnp.zeros((width - near, side), jnp.float32)
    running = products(far_ref, far_sums, 0, chunks // 2, zeros)

    def hand_on(block):
        return remote(
            feat_ref.at[block],
            feat_ref.at[block],
            hand_sem.at[block],
            feat_recv_sem.at[block],
            (mate_of(my_outer) * inner + my_inner, col),
        )

    other_pair = [2 * (1 - lax.div(my_outer, 2)), 2 * (1 - lax.div(my_outer, 2)) + 1]
    if line:

        @pl.when(near_end == 1)
        def _():
            for block in other_pair:
                arrived(feat_ref.at[block], feat_recv_sem.at[block])
                hand_on(block).start()

    products(far_ref, far_sums, chunks // 2, chunks, running)
    for index, block in enumerate(order):
        for peer in others(my_inner, inner):
            pack(far_sums, strips[1], block * inner + peer)
        if index < 2:
            for copy in pair_sends(outer + index):
                copy.start()
    for block in order:
        pack(near_sums, strips[0], block * inner + my_inner)
        pack(far_sums, strips[1], block * inner + my_inner)
    values = []
    near_pairs = []
    grads = [0.0] * 2
    for step, (block, half) in enumerate(steps):
        for copy in pair_sends(step):
            copy.wait_send()
        if outer <= step < len(steps) - 2:
            for copy in pair_sends(step + 2):
                copy.start()
        value = part_ref[block * inner + my_inner, strip(half)].astype(jnp.float32)
        for peer in others(my_inner, inner):
            arrived(pair_recv.at[peer, block, strip(half)], pair_recv_sem.at[peer, block, half])
            value += pair_recv[peer, block, strip(half)].astype(jnp.float32)
        rounded = value.astype(jnp.bfloat16)
        if block is my_outer:
            values.append(value)
        else:
            pair_sum[block, strip(half)] = rounded
            start(
                remote(
                    pair_sum.at[block, strip(half)],
                    line_recv.at[my_outer, strip(half)],
                    line_send_sem.at[block, half],
                    line_recv_sem.at[my_outer, half],
                    (block * inner + my_inner, col),
                )
            )
        if half == 0:
            near_pairs.append(rounded)
            continue
        if block is not my_outer:
            if line and block is not outer_mate:

                @pl.when(near_end == 0)
                def _(block=block):
                    arrived(feat_ref.at[block], feat_recv_sem.at[block])

            else:
                arrived(feat_ref.at[block], feat_recv_sem.at[block])
        for index, pairs in enumerate([near_pairs[step - outer], rounded]):
            grads[index] += jnp.dot(pairs, feat_ref[block], preferred_element_type=jnp.float32)
    turned = jnp.concatenate(grads, axis=0)
    for position in range(cols):
        whole_grad[lines_of(lax.rem(position + first, cols)), :] = turned[
            position * own_width : (position + 1) * own_width
        ]
    local_grad[...] = whole_grad[...].T
    piece = local_grad.shape[0] // cols

    def rows_of(ref, index):
        return ref.at[pl.ds(pl.multiple_of(index * piece, piece), piece)]

    for peer in others(col, cols):
        start(
            remote(
                rows_of(local_grad, peer),
                col_recv.at[col],
                col_send_sem.at[peer],
                col_recv_sem.at[col],
                (row, peer),
            )
        )
    piece_sum = rows_of(local_grad, col)[...]
    for peer in others(col, cols):
        arrived(col_recv.at[peer], col_recv_sem.at[peer])
        piece_sum += col_recv[peer]
    row_recv[row] = piece_sum.astype(jnp.bfloat16)
    for peer in others(row, rows):
        start(
            remote(
                row_recv.at[row],
                row_recv.at[row],
                row_send_sem.at[peer],
                row_recv_sem.at[row],
                (peer, col),
            )
        )
    for half in range(2):
        for peer in reversed(order[:-1]):
            arrived(line_recv.at[peer, strip(half)], line_recv_sem.at[peer, half])
            values[half] += line_recv[peer, strip(half)].astype(jnp.float32)
    turned = jnp.concatenate(values, axis=0).astype(jnp.bfloat16)
    for position in range(cols):
        aggregate[lines_of(lax.rem(position + first, cols)), :] = turned[
            position * own_width : (position + 1) * own_width
        ]
    node_out_ref[...] = (
        jnp.dot(weight_ref[...], aggregate[...], preferred_element_type=jnp.float32)
        .T.astype(jnp.bfloat16)
    )
    node_store = pltpu.make_async_copy(node_out_ref, node_out_hbm, store_sem.at[0])
    node_store.start()
    for peer in others(row, rows):
        arrived(row_recv.at[peer], row_recv_sem.at[peer])
    piece_sum = row_recv[0].astype(jnp.float32)
    for index in range(1, rows):
        piece_sum += row_recv[index].astype(jnp.float32)
    rows_of(whole_grad, col)[...] = piece_sum
    for peer in others(col, cols):
        start(
            remote(
                rows_of(whole_grad, col),
                rows_of(whole_grad, col),
                all_send_sem.at[peer],
                all_recv_sem.at[col],
                (row, peer),
            )
        )
    for peer in others(col, cols):
        arrived(rows_of(whole_grad, peer), all_recv_sem.at[peer])
    weight_store = pltpu.make_async_copy(whole_grad, weight_out_hbm, store_sem.at[1])
    weight_store.start()
    for copy in sends:
        copy.wait_send()
    if line:

        @pl.when(near_end == 1)
        def _():
            for block in other_pair:
                hand_on(block).wait_send()

    node_store.wait()
    weight_store.wait()


def finish_kernel(
    node_hbm, grad_hbm, imp_hbm, delta_hbm, node_out, imp_out, node_ref, grad_ref, imp_ref, delta_ref, sems
):
    loads = [
        pltpu.make_async_copy(source, target, sems.at[index])
        for index, (source, target) in enumerate(
            [(node_hbm, node_ref), (grad_hbm, grad_ref), (imp_hbm, imp_ref), (delta_hbm, delta_ref)]
        )
    ]
    for load in loads:
        load.start()
    loads[0].wait()
    node_store = pltpu.make_async_copy(node_ref, node_out, sems.at[4])
    node_store.start()
    for load in loads[1:]:
        load.wait()
    imp_ref[...] = imp_ref[...] - grad_ref[...] * delta_ref[...]
    imp_store = pltpu.make_async_copy(imp_ref, imp_out, sems.at[5])
    imp_store.start()
    node_store.wait()
    imp_store.wait()


def local(
    rows,
    cols,
    tile_vals,
    tile_row,
    tile_col,
    tile_count,
    out_grad,
    relu_mask,
    features,
    weight,
    importance,
    weight_delta,
):
    slots, side = tile_vals.shape[2], tile_vals.shape[-1]
    nodes, depth = features.shape
    block_nodes, own_width = out_grad.shape
    width = own_width * cols
    inner = 2 if rows % 2 == 0 else 1
    outer = rows // inner
    params = functools.partial(pltpu.CompilerParams, vmem_limit_bytes=60 * 2**20)
    dma = pltpu.SemaphoreType.DMA
    piece = depth // cols
    bf16 = jnp.bfloat16
    f32 = jnp.float32
    i32 = jnp.int32

    node_grad, weight_grad = pl.pallas_call(
        functools.partial(layer_kernel, outer, inner, cols),
        out_shape=(
            jax.ShapeDtypeStruct((nodes, depth), bf16),
            jax.ShapeDtypeStruct((depth, width), f32),
        ),
        in_specs=[HBM, HBM, SMEM] + [HBM] * 5,
        out_specs=(HBM, HBM),
        scratch_shapes=[
            pltpu.VMEM((own_width, block_nodes), bf16),
            pltpu.VMEM((own_width, block_nodes), i32),
            pltpu.VMEM((block_nodes // side, 2 * own_width, side), bf16),
            pltpu.VMEM((block_nodes // side, width - 2 * own_width, side), bf16),
            pltpu.VMEM((slots, side, side), bf16),
            pltpu.VMEM((1, slots), i32),
            pltpu.VMEM((1, slots), i32),
            pltpu.VMEM((8, slots), i32),
            pltpu.SMEM((8, slots), i32),
            pltpu.VMEM((slots, 2 * own_width, side), bf16),
            pltpu.VMEM((slots, width - 2 * own_width, side), bf16),
            pltpu.VMEM((rows, width, nodes), bf16),
            pltpu.VMEM((outer, nodes, depth), bf16),
            pltpu.VMEM((depth, width), bf16),
            pltpu.VMEM((nodes, depth), bf16),
            pltpu.VMEM((inner, outer, width, nodes), bf16),
            pltpu.VMEM((outer, width, nodes), bf16),
            pltpu.VMEM((outer, width, nodes), bf16),
            pltpu.VMEM((depth, width), f32),
            pltpu.VMEM((cols, piece, width), f32),
            pltpu.VMEM((rows, piece, width), bf16),
            pltpu.VMEM((depth, width), f32),
            pltpu.VMEM((width, nodes), bf16),
            dma((6,)),
            dma((slots // CHUNK,)),
            dma((1,)),
            dma((2,)),
            dma((cols, PARTS)),
            dma((cols, PARTS)),
            dma((cols, PARTS)),
            dma((inner, outer, 2)),
            dma((inner, outer, 2)),
            dma((outer, 2)),
            dma((outer, 2)),
            dma((cols,)),
            dma((cols,)),
            dma((rows,)),
            dma((rows,)),
            dma((cols,)),
            dma((cols,)),
            dma((outer,)),
            dma((outer,)),
            dma((outer,)),
        ],
        compiler_params=params(collective_id=0, has_side_effects=True),
        name="layer_backward",
    )(
        tile_row.reshape(1, slots),
        tile_col.reshape(1, slots),
        tile_count,
        out_grad.T,
        relu_mask.T,
        tile_vals.reshape(slots, side, side),
        features,
        weight,
    )

    return pl.pallas_call(
        finish_kernel,
        out_shape=(
            jax.ShapeDtypeStruct((nodes, depth), bf16),
            jax.ShapeDtypeStruct((depth, width), f32),
        ),
        in_specs=[HBM] * 4,
        out_specs=(HBM, HBM),
        scratch_shapes=[
            pltpu.VMEM((nodes, depth), bf16),
            pltpu.VMEM((depth, width), f32),
            pltpu.VMEM((depth, width), f32),
            pltpu.VMEM((depth, width), f32),
            dma((6,)),
        ],
        compiler_params=params(),
        name="finish",
    )(node_grad, weight_grad, importance, weight_delta)


def solution(mesh):
    return jax.shard_map(
        functools.partial(local, mesh.shape["row"], mesh.shape["col"]),
        mesh=mesh,
        in_specs=(
            P("row", "col", None, None, None),
            P("row", "col", None),
            P("row", "col", None),
            P("row", "col"),
            P("row", "col"),
            P("row", "col"),
            P(("row", "col"), None),
            P(),
            P(),
            P(),
        ),
        out_specs=(P(("row", "col"), None), P()),
        check_vma=False,
    )
```

```python
import functools

import jax
import jax.numpy as jnp
from jax import lax
from jax.experimental import pallas as pl
from jax.experimental.pallas import tpu as pltpu
from jax.sharding import PartitionSpec as P

MESH = pl.DeviceIdType.MESH
SMEM = pl.BlockSpec(memory_space=pltpu.SMEM)
HBM = pl.BlockSpec(memory_space=pltpu.HBM)
PARTS = 4
CHUNK = 16


def remote(src, dst, send_sem, recv_sem, device):
    return pltpu.make_async_remote_copy(
        src_ref=src,
        dst_ref=dst,
        send_sem=send_sem,
        recv_sem=recv_sem,
        device_id=device,
        device_id_type=MESH,
    )


def others(me, count):
    return [lax.rem(me + step, count) for step in range(1, count)]


def mate_of(index):
    return index + 1 - 2 * lax.rem(index, 2)


def sort_tables(cols, rows, count, columns):
    slots = cols.shape[1]
    shape = (slots, slots)
    lane = lax.broadcasted_iota(jnp.int32, shape, 1)
    sublane = lax.broadcasted_iota(jnp.int32, shape, 0)
    diagonal = lane == sublane
    here = jnp.broadcast_to(cols, shape)
    key = jnp.where(lane < count, here, columns)

    def upright(value):
        return jnp.sum(jnp.where(diagonal, value, 0), axis=1, keepdims=True)

    mine = upright(key)
    row = upright(jnp.broadcast_to(rows, shape))
    earlier = (key == mine) & (lane < sublane)
    rank = jnp.sum(jnp.where((key < mine) | earlier, 1, 0), axis=1, keepdims=True)
    keep = jnp.max(jnp.where(earlier, 1, 0), axis=1, keepdims=True)
    placed = rank == lane

    def in_order(value):
        return jnp.sum(jnp.where(placed, value, 0), axis=0, keepdims=True)

    first = jnp.sum(jnp.where(mine < lane, 1, 0), axis=0, keepdims=True)
    last = jnp.sum(jnp.where(mine <= lane, 1, 0), axis=0, keepdims=True)
    return in_order(sublane), in_order(row), in_order(keep), first, last


def layer_kernel(
    outer,
    inner,
    cols,
    rows_hbm,
    cols_hbm,
    count_ref,
    grad_hbm,
    mask_hbm,
    vals_hbm,
    feat_hbm,
    weight_hbm,
    node_out_hbm,
    weight_out_hbm,
    grad_ref,
    mask_ref,
    near_ref,
    far_ref,
    held,
    tile_rows_ref,
    tile_cols_ref,
    table_ref,
    table,
    near_sums,
    far_sums,
    part_ref,
    feat_ref,
    weight_ref,
    node_out_ref,
    pair_recv,
    pair_sum,
    line_recv,
    local_grad,
    col_recv,
    row_recv,
    whole_grad,
    aggregate,
    load_sem,
    tile_sem,
    table_sem,
    store_sem,
    send_sem,
    pass_sem,
    recv_sem,
    pair_send_sem,
    pair_recv_sem,
    line_send_sem,
    line_recv_sem,
    col_send_sem,
    col_recv_sem,
    row_send_sem,
    row_recv_sem,
    all_send_sem,
    all_recv_sem,
    feat_send_sem,
    feat_recv_sem,
):
    row, col = lax.axis_index("row"), lax.axis_index("col")
    rows = outer * inner
    my_outer, my_inner = lax.div(row, inner), lax.rem(row, inner)
    slots, side = held.shape[0], held.shape[-1]
    width, nodes = part_ref.shape[1:]
    per_block = nodes // side
    columns = rows * per_block
    sends = []

    def start(copy):
        copy.start()
        sends.append(copy)

    def arrived(slot, sem):
        remote(slot, slot, sem, sem, (row, mate_of(col))).wait_recv()

    if outer == 4:
        across = lax.rem(my_outer + 2, outer)
        order = [across, mate_of(across), mate_of(my_outer), my_outer]
    else:
        order = others(my_outer, outer) + [my_outer]

    loads = [
        pltpu.make_async_copy(source, target, load_sem.at[index])
        for index, (source, target) in enumerate(
            [
                (grad_hbm, grad_ref),
                (mask_hbm, mask_ref),
                (rows_hbm, tile_rows_ref),
                (cols_hbm, tile_cols_ref),
                (feat_hbm, feat_ref.at[my_outer]),
                (weight_hbm, weight_ref),
            ]
        )
    ]
    for load in loads:
        load.start()
    tile_loads = []
    for index in range(slots // CHUNK):
        piece = pl.ds(index * CHUNK, CHUNK)
        load = pltpu.make_async_copy(vals_hbm.at[piece], held.at[piece], tile_sem.at[index])
        load.start()
        tile_loads.append(load)
    partners = [(row, peer) for peer in others(col, cols)] + [
        (peer, col) for peer in others(row, rows)
    ]
    barrier = pltpu.get_barrier_semaphore()
    for partner in partners:
        pl.semaphore_signal(barrier, inc=1, device_id=partner, device_id_type=MESH)

    loads[2].wait()
    loads[3].wait()
    for index, line in enumerate(
        sort_tables(tile_cols_ref[...], tile_rows_ref[...], count_ref[0, 0], columns)
    ):
        table_ref[index : index + 1, :] = line
    to_scalars = pltpu.make_async_copy(table_ref, table, table_sem.at[0])
    to_scalars.start()

    loads[0].wait()
    loads[1].wait()
    mate = mate_of(col)
    first = col - lax.rem(col, 2)
    far = [lax.rem(col + 2 * step, cols) for step in range(1, cols // 2)]
    row_tiles = near_ref.shape[0]
    size = row_tiles // PARTS
    own_width = grad_ref.shape[0]

    def tiles_of(part):
        return pl.ds(part * size, size)

    def lines_of(position):
        return pl.ds(pl.multiple_of(position * own_width, own_width), own_width)

    def near_piece(block, part):
        return near_ref.at[tiles_of(part), lines_of(lax.rem(block, 2))]

    def far_piece(block, part, device):
        position = lax.rem(block - (device - lax.rem(device, 2)) + cols, cols) - 2
        return far_ref.at[tiles_of(part), lines_of(position)]

    for tile in range(row_tiles):
        lanes = slice(tile * side, (tile + 1) * side)
        near_ref[tile, lines_of(lax.rem(col, 2)), :] = (
            grad_ref[:, lanes].astype(jnp.float32) * mask_ref[:, lanes].astype(jnp.float32)
        ).astype(jnp.bfloat16)
    pl.semaphore_wait(barrier, len(partners))
    for part in range(PARTS):
        for peer in far:
            start(
                remote(
                    near_piece(col, part),
                    far_piece(col, part, peer),
                    send_sem.at[peer, part],
                    recv_sem.at[col, part],
                    (row, peer),
                )
            )
        ref = near_piece(col, part)
        start(remote(ref, ref, send_sem.at[mate, part], recv_sem.at[col, part], (row, mate)))
    for peer in order[:-1]:
        start(
            remote(
                feat_hbm,
                feat_ref.at[my_outer],
                feat_send_sem.at[peer],
                feat_recv_sem.at[my_outer],
                (peer * inner + my_inner, col),
            )
        )

    def products(masked_ref, sums, begin, end, running):
        def chunk_step(index, running):
            for step in range(CHUNK):
                place = index * CHUNK + step
                product = jnp.dot(
                    masked_ref[table[1, place]],
                    held[table[0, place]],
                    preferred_element_type=jnp.float32,
                )
                running = running * table[2, place].astype(jnp.float32) + product
                sums[place] = running.astype(jnp.bfloat16)
            return running

        return lax.fori_loop(begin, end, chunk_step, running)

    near = near_ref.shape[1]
    strips = [pl.ds(0, near), pl.ds(near, width - near)]

    def pack(sums, strip, block):
        for part in range(per_block):
            column = block * per_block + part
            begin, end = table[3, column], table[4, column]
            used = jnp.minimum(end - begin, 1).astype(jnp.float32)
            value = sums[jnp.maximum(end - 1, 0)].astype(jnp.float32) * used
            part_ref[block, strip, part * side : (part + 1) * side] = value.astype(jnp.bfloat16)

    to_scalars.wait()
    for load in tile_loads + loads[4:]:
        load.wait()
    for part in range(PARTS):
        arrived(near_piece(mate, part), recv_sem.at[mate, part])
    chunks = slots // CHUNK
    pause = chunks * 3 // 4
    zeros = jnp.zeros((near, side), jnp.float32)
    running = products(near_ref, near_sums, 0, pause, zeros)
    for part in range(PARTS):
        for peer in far:
            ref = far_piece(peer, part, col)
            arrived(ref, recv_sem.at[peer, part])
            start(remote(ref, ref, pass_sem.at[peer, part], recv_sem.at[peer, part], (row, mate)))
    products(near_ref, near_sums, pause, chunks, running)

    steps = [(block, half) for half in range(2) for block in order]

    def strip(half):
        return strips[half]

    def pair_sends(step):
        block, half = steps[step]
        return [
            remote(
                part_ref.at[block * inner + peer, strip(half)],
                pair_recv.at[my_inner, block, strip(half)],
                pair_send_sem.at[peer, block, half],
                pair_recv_sem.at[my_inner, block, half],
                (my_outer * inner + peer, col),
            )
            for peer in others(my_inner, inner)
        ]

    for step, block in enumerate(order):
        for peer in others(my_inner, inner):
            pack(near_sums, strips[0], block * inner + peer)
        for copy in pair_sends(step):
            copy.start()
    for part in range(PARTS):
        for peer in far:
            block = mate_of(peer)
            arrived(far_piece(block, part, col), recv_sem.at[block, part])
    products(far_ref, far_sums, 0, chunks, jnp.zeros((width - near, side), jnp.float32))
    for index, block in enumerate(order):
        for peer in others(my_inner, inner):
            pack(far_sums, strips[1], block * inner + peer)
        if index < 2:
            for copy in pair_sends(outer + index):
                copy.start()
    for block in order:
        pack(near_sums, strips[0], block * inner + my_inner)
        pack(far_sums, strips[1], block * inner + my_inner)
    values = []
    near_pairs = []
    grads = [0.0] * 2
    for step, (block, half) in enumerate(steps):
        for copy in pair_sends(step):
            copy.wait_send()
        if outer <= step < len(steps) - 2:
            for copy in pair_sends(step + 2):
                copy.start()
        value = part_ref[block * inner + my_inner, strip(half)].astype(jnp.float32)
        for peer in others(my_inner, inner):
            arrived(pair_recv.at[peer, block, strip(half)], pair_recv_sem.at[peer, block, half])
            value += pair_recv[peer, block, strip(half)].astype(jnp.float32)
        rounded = value.astype(jnp.bfloat16)
        if block is my_outer:
            values.append(value)
        else:
            pair_sum[block, strip(half)] = rounded
            start(
                remote(
                    pair_sum.at[block, strip(half)],
                    line_recv.at[my_outer, strip(half)],
                    line_send_sem.at[block, half],
                    line_recv_sem.at[my_outer, half],
                    (block * inner + my_inner, col),
                )
            )
        if half == 0:
            near_pairs.append(rounded)
            continue
        if block is not my_outer:
            arrived(feat_ref.at[block], feat_recv_sem.at[block])
        for index, pairs in enumerate([near_pairs[step - outer], rounded]):
            grads[index] += jnp.dot(pairs, feat_ref[block], preferred_element_type=jnp.float32)
    turned = jnp.concatenate(grads, axis=0)
    for position in range(cols):
        whole_grad[lines_of(lax.rem(position + first, cols)), :] = turned[
            position * own_width : (position + 1) * own_width
        ]
    local_grad[...] = whole_grad[...].T
    piece = local_grad.shape[0] // cols

    def rows_of(ref, index):
        return ref.at[pl.ds(pl.multiple_of(index * piece, piece), piece)]

    for peer in others(col, cols):
        start(
            remote(
                rows_of(local_grad, peer),
                col_recv.at[col],
                col_send_sem.at[peer],
                col_recv_sem.at[col],
                (row, peer),
            )
        )
    piece_sum = rows_of(local_grad, col)[...]
    for peer in others(col, cols):
        arrived(col_recv.at[peer], col_recv_sem.at[peer])
        piece_sum += col_recv[peer]
    row_recv[row] = piece_sum.astype(jnp.bfloat16)
    for peer in others(row, rows):
        start(
            remote(
                row_recv.at[row],
                row_recv.at[row],
                row_send_sem.at[peer],
                row_recv_sem.at[row],
                (peer, col),
            )
        )
    for half in range(2):
        for peer in reversed(order[:-1]):
            arrived(line_recv.at[peer, strip(half)], line_recv_sem.at[peer, half])
            values[half] += line_recv[peer, strip(half)].astype(jnp.float32)
    turned = jnp.concatenate(values, axis=0).astype(jnp.bfloat16)
    for position in range(cols):
        aggregate[lines_of(lax.rem(position + first, cols)), :] = turned[
            position * own_width : (position + 1) * own_width
        ]
    node_out_ref[...] = (
        jnp.dot(weight_ref[...], aggregate[...], preferred_element_type=jnp.float32)
        .T.astype(jnp.bfloat16)
    )
    node_store = pltpu.make_async_copy(node_out_ref, node_out_hbm, store_sem.at[0])
    node_store.start()
    for peer in others(row, rows):
        arrived(row_recv.at[peer], row_recv_sem.at[peer])
    piece_sum = row_recv[0].astype(jnp.float32)
    for index in range(1, rows):
        piece_sum += row_recv[index].astype(jnp.float32)
    rows_of(whole_grad, col)[...] = piece_sum
    for peer in others(col, cols):
        start(
            remote(
                rows_of(whole_grad, col),
                rows_of(whole_grad, col),
                all_send_sem.at[peer],
                all_recv_sem.at[col],
                (row, peer),
            )
        )
    for peer in others(col, cols):
        arrived(rows_of(whole_grad, peer), all_recv_sem.at[peer])
    weight_store = pltpu.make_async_copy(whole_grad, weight_out_hbm, store_sem.at[1])
    weight_store.start()
    for copy in sends:
        copy.wait_send()
    node_store.wait()
    weight_store.wait()


def finish_kernel(
    node_hbm, grad_hbm, imp_hbm, delta_hbm, node_out, imp_out, node_ref, grad_ref, imp_ref, delta_ref, sems
):
    loads = [
        pltpu.make_async_copy(source, target, sems.at[index])
        for index, (source, target) in enumerate(
            [(node_hbm, node_ref), (grad_hbm, grad_ref), (imp_hbm, imp_ref), (delta_hbm, delta_ref)]
        )
    ]
    for load in loads:
        load.start()
    loads[0].wait()
    node_store = pltpu.make_async_copy(node_ref, node_out, sems.at[4])
    node_store.start()
    for load in loads[1:]:
        load.wait()
    imp_ref[...] = imp_ref[...] - grad_ref[...] * delta_ref[...]
    imp_store = pltpu.make_async_copy(imp_ref, imp_out, sems.at[5])
    imp_store.start()
    node_store.wait()
    imp_store.wait()


def local(
    rows,
    cols,
    tile_vals,
    tile_row,
    tile_col,
    tile_count,
    out_grad,
    relu_mask,
    features,
    weight,
    importance,
    weight_delta,
):
    slots, side = tile_vals.shape[2], tile_vals.shape[-1]
    nodes, depth = features.shape
    block_nodes, own_width = out_grad.shape
    width = own_width * cols
    inner = 2 if rows % 2 == 0 else 1
    outer = rows // inner
    params = functools.partial(pltpu.CompilerParams, vmem_limit_bytes=60 * 2**20)
    dma = pltpu.SemaphoreType.DMA
    piece = depth // cols
    bf16 = jnp.bfloat16
    f32 = jnp.float32
    i32 = jnp.int32

    node_grad, weight_grad = pl.pallas_call(
        functools.partial(layer_kernel, outer, inner, cols),
        out_shape=(
            jax.ShapeDtypeStruct((nodes, depth), bf16),
            jax.ShapeDtypeStruct((depth, width), f32),
        ),
        in_specs=[HBM, HBM, SMEM] + [HBM] * 5,
        out_specs=(HBM, HBM),
        scratch_shapes=[
            pltpu.VMEM((own_width, block_nodes), bf16),
            pltpu.VMEM((own_width, block_nodes), i32),
            pltpu.VMEM((block_nodes // side, 2 * own_width, side), bf16),
            pltpu.VMEM((block_nodes // side, width - 2 * own_width, side), bf16),
            pltpu.VMEM((slots, side, side), bf16),
            pltpu.VMEM((1, slots), i32),
            pltpu.VMEM((1, slots), i32),
            pltpu.VMEM((8, slots), i32),
            pltpu.SMEM((8, slots), i32),
            pltpu.VMEM((slots, 2 * own_width, side), bf16),
            pltpu.VMEM((slots, width - 2 * own_width, side), bf16),
            pltpu.VMEM((rows, width, nodes), bf16),
            pltpu.VMEM((outer, nodes, depth), bf16),
            pltpu.VMEM((depth, width), bf16),
            pltpu.VMEM((nodes, depth), bf16),
            pltpu.VMEM((inner, outer, width, nodes), bf16),
            pltpu.VMEM((outer, width, nodes), bf16),
            pltpu.VMEM((outer, width, nodes), bf16),
            pltpu.VMEM((depth, width), f32),
            pltpu.VMEM((cols, piece, width), f32),
            pltpu.VMEM((rows, piece, width), bf16),
            pltpu.VMEM((depth, width), f32),
            pltpu.VMEM((width, nodes), bf16),
            dma((6,)),
            dma((slots // CHUNK,)),
            dma((1,)),
            dma((2,)),
            dma((cols, PARTS)),
            dma((cols, PARTS)),
            dma((cols, PARTS)),
            dma((inner, outer, 2)),
            dma((inner, outer, 2)),
            dma((outer, 2)),
            dma((outer, 2)),
            dma((cols,)),
            dma((cols,)),
            dma((rows,)),
            dma((rows,)),
            dma((cols,)),
            dma((cols,)),
            dma((outer,)),
            dma((outer,)),
        ],
        compiler_params=params(collective_id=0, has_side_effects=True),
        name="layer_backward",
    )(
        tile_row.reshape(1, slots),
        tile_col.reshape(1, slots),
        tile_count,
        out_grad.T,
        relu_mask.T,
        tile_vals.reshape(slots, side, side),
        features,
        weight,
    )

    return pl.pallas_call(
        finish_kernel,
        out_shape=(
            jax.ShapeDtypeStruct((nodes, depth), bf16),
            jax.ShapeDtypeStruct((depth, width), f32),
        ),
        in_specs=[HBM] * 4,
        out_specs=(HBM, HBM),
        scratch_shapes=[
            pltpu.VMEM((nodes, depth), bf16),
            pltpu.VMEM((depth, width), f32),
            pltpu.VMEM((depth, width), f32),
            pltpu.VMEM((depth, width), f32),
            dma((6,)),
        ],
        compiler_params=params(),
        name="finish",
    )(node_grad, weight_grad, importance, weight_delta)


def solution(mesh):
    return jax.shard_map(
        functools.partial(local, mesh.shape["row"], mesh.shape["col"]),
        mesh=mesh,
        in_specs=(
            P("row", "col", None, None, None),
            P("row", "col", None),
            P("row", "col", None),
            P("row", "col"),
            P("row", "col"),
            P("row", "col"),
            P(("row", "col"), None),
            P(),
            P(),
            P(),
        ),
        out_specs=(P(("row", "col"), None), P()),
        check_vma=False,
    )
```
